256 devices in a mesh: ctx: 32 (over x, z_hi, core), exp: 8 (over y, z_lo).
Axes of the slice: x: 4, y: 4, z: 8 (z_hi: 4, z_lo: 2; z = z_hi * 2 + z_lo), core: 2. Of those that a mesh axis runs over, the one named last changes fastest.
Arguments:
- tokens: bfloat16 [4096, 2880], P('ctx'), may hold values from -6 to 6
- positions: int32 [4096], P('ctx'), may hold values from 0 to 4095, as said below
- norm_attn: float32 [2880], replicated, may hold values from 0.5 to 1.5
- norm_moe: float32 [2880], replicated, may hold values from 0.5 to 1.5
- w_query: bfloat16 [2880, 4096], P(None, 'exp')
- key_matrix: bfloat16 [2880, 512], P(None, 'exp'), may hold values from -0.109375 to 0.109375
- value_matrix: bfloat16 [2880, 512], P(None, 'exp'), may hold values from -0.109375 to 0.109375
- w_out: bfloat16 [4096, 2880], P('exp'), may hold values from -0.09375 to 0.09375
- sinks: float32 [64], P('exp'), may hold values from 6 to 13
- expert_ids: int32 [4096, 4], P('ctx'), may hold values from 0 to 31, all different within a row; in each aligned block of 128 rows (0 to 127, 128 to 255, ...) at most 24 rows name the same one
- expert_weights: float32 [4096, 4], P('ctx'), may hold values from 0.1 to 0.6
- w_gate: bfloat16 [32, 2880, 1440], P('ctx', None, 'exp'), may hold values from -0.109375 to 0.109375
- w_up: bfloat16 [32, 2880, 1440], P('ctx', None, 'exp'), may hold values from -0.109375 to 0.109375
- w_down: bfloat16 [32, 1440, 2880], P('ctx', 'exp'), may hold values from -0.15625 to 0.15625
Outputs:
- attended: bfloat16 [4096, 2880], P(('ctx', 'exp'))
- layer_out: bfloat16 [4096, 2880], P(('ctx', 'exp'))
The draws below stay inside these ranges and needn't reach their ends.
Inputs may be any that keep to these rules, and one draw needn't show every extreme that they name: `positions`: a permutation of 0 to 4095; each aligned run of 128 rows holds 128 consecutive positions in increasing order. `expert_ids`: the 4 experts of a row differ; in each aligned block of 128 rows no expert is named by more than 24 rows, a bound that some block reaches.
All inputs are finite; a program needn't handle non-finite values.
Results may differ from the reference program's by a relative error of at most 0.02.
The reference program's roundings to bfloat16 on the way count: a program that leaves them out, or rounds other values in their place, can miss the bound.
Values may be sent and summed in bfloat16 or wider, within the bound.
No kernel may reach another device: no remote copies, remote signals or barrier semaphores. Data moves between devices by JAX's collectives and lax.ppermute only.
A program may use at most 128 MiB of HBM per device.

```python
import math
import jax
import jax.numpy as jnp
import numpy as np
from jax import lax

MODEL_WIDTH = 2880
QUERY_HEADS = 64
KEY_VALUE_HEADS = 8
HEAD_WIDTH = 64
TOP = 4
FFE = 1440
SHARD_TOKENS = 128
BLOCK = 128
EXPERTS = 32
SEQUENCE_TOKENS = 4096
CAP = 24
N_EXP = 8


def draw_positions(key, part):
    key = jax.random.fold_in(key, 5)
    order = jax.random.permutation(key, SEQUENCE_TOKENS // BLOCK).astype(jnp.int32)
    within = jnp.arange(BLOCK).astype(jnp.int32)
    return (order[:, None] * BLOCK + within[None, :]).reshape(SEQUENCE_TOKENS).astype(jnp.int32)


def draw_w_query(key, part):
    key = jax.random.fold_in(key, 11)
    base_key = jax.random.fold_in(key, 0)
    base = jax.random.normal(base_key, (MODEL_WIDTH, QUERY_HEADS * HEAD_WIDTH), jnp.float32)
    head_scale = jnp.full((QUERY_HEADS,), 2.0, jnp.float32)
    column_scale = jnp.repeat(head_scale, HEAD_WIDTH)
    return (base * column_scale[None, :] * MODEL_WIDTH ** (-0.5)).astype(jnp.bfloat16)


def block_scale(key, dims, pieces, low, high):
    def one(position, parts):
        heights = jax.random.uniform(jax.random.fold_in(jax.random.fold_in(key, 6), position), (parts,), jnp.float32, low / len(pieces), high / len(pieces))
        return jnp.repeat(jnp.exp(heights), dims[position] // parts).reshape((-1,) + (1,) * (len(dims) - position - 1))

    gain = one(*pieces[0])
    for cut in pieces[1:]:
        gain = gain * one(*cut)
    return gain


def assign_block(stream_key, own, number, rows, count, top, most, slope):
    sequence = jax.random.permutation(stream_key, count)
    heavy_load, usual = portions_of(count, rows * top, most, slope, True), portions_of(count, rows * top, most, slope, False)
    places = jnp.arange(count)

    def named(lengths, offset_by):
        used = int((lengths > 0).sum())
        fixed = max(1, used // 4)
        shifted = fixed + (places - fixed + offset_by * (used - fixed)) % max(1, count - fixed)
        return jnp.zeros((count,), jnp.int32).at[sequence[jnp.where(places < fixed, places, shifted)]].set(jnp.asarray(lengths, jnp.int32))

    lengths = jnp.where(number % 4 == 0, named(heavy_load, number // 4), named(usual, number - number // 4 - 1))
    mixed = jax.random.permutation(jax.random.fold_in(own, 3), count)
    donor, sink = mixed[0:count // 2 * 2:2], mixed[1:count // 2 * 2:2]
    margin = jnp.minimum(lengths[donor] - 1, most - lengths[sink]) // 2
    margin = jnp.where((donor == sequence[0]) | (sink == sequence[0]) | (lengths[sink] == 0), 0, jnp.maximum(margin, 0))
    shifted = jax.random.randint(jax.random.fold_in(own, 4), (count // 2,), 0, 1 << 20) % (margin + 1)
    lengths = lengths.at[donor].add(-shifted).at[sink].add(shifted)
    members = jnp.searchsorted(jnp.cumsum(lengths), jnp.arange(rows * top), side="right").astype(jnp.int32)
    table = members.reshape(top, rows).T
    table = table[jax.random.permutation(jax.random.fold_in(own, 1), rows)]
    offset_by = jax.random.randint(jax.random.fold_in(own, 2), (rows, 1), 0, top)
    return jnp.take_along_axis(table, (jnp.arange(top)[None, :] + offset_by) % top, axis=1)


def portions_of(number_of, total, bound, skew, full):
    loads = [(1 << 20) // math.isqrt(standing ** skew) + 1 for standing in range(1, number_of + 1)]
    largest = bound if full else min(bound, max(-(-total // number_of), total * loads[0] // sum(loads)))
    least = 1 if total - largest >= number_of - 1 else 0
    counts, rest = [largest] + [least] * (number_of - 1), total - largest - least * (number_of - 1)
    while rest > 0:
        free = [i for i in range(1, number_of) if counts[i] < largest] or [i for i in range(1, number_of) if counts[i] < bound]
        whole, remaining = sum([loads[i] for i in free]), rest
        for i in free:
            extra = min(bound - counts[i], max(1, remaining * loads[i] // whole), rest)
            counts[i] = counts[i] + extra
            rest = rest - extra
    return np.array(counts)


def bell_draw(stream_key, dims, width, most, shards=(), held_as=jnp.bfloat16):
    values = jax.random.normal(stream_key, dims, jnp.float32) * width
    if len(shards) > 0:
        values = block_scale(stream_key, dims, shards, -0.22, 0.18) * values
    return jnp.clip(values, min=-most, max=most).astype(held_as)


def setup_inputs(seed: int = 0) -> dict:
    arg_keys = jax.random.split(jax.random.key(seed), 15)
    tokens = bell_draw(arg_keys[0], (SEQUENCE_TOKENS, MODEL_WIDTH), 1.0, 6.0, ((0, 32),))
    positions = draw_positions(jax.random.fold_in(arg_keys[14], 71), 0)
    norm_attn = jnp.clip(1.0 + 0.1 * jax.random.normal(arg_keys[2], (MODEL_WIDTH,), jnp.float32), 0.5, 1.5)
    norm_moe = jnp.clip(1.0 + 0.1 * jax.random.normal(arg_keys[3], (MODEL_WIDTH,), jnp.float32), 0.5, 1.5)
    w_query = draw_w_query(jax.random.fold_in(arg_keys[14], 71), 0)
    key_matrix = bell_draw(arg_keys[5], (MODEL_WIDTH, KEY_VALUE_HEADS * HEAD_WIDTH), MODEL_WIDTH ** -0.5, 0.109375, ((1, 8),))
    value_matrix = bell_draw(arg_keys[6], (MODEL_WIDTH, KEY_VALUE_HEADS * HEAD_WIDTH), MODEL_WIDTH ** -0.5, 0.109375, ((1, 8),))
    w_out = bell_draw(arg_keys[7], (QUERY_HEADS * HEAD_WIDTH, MODEL_WIDTH), (QUERY_HEADS * HEAD_WIDTH) ** -0.5, 0.09375, ((0, 8),))
    sinks = jnp.clip(6.0 + 7.0 * jax.random.uniform(arg_keys[8], (QUERY_HEADS,), jnp.float32) ** block_scale(arg_keys[8], (QUERY_HEADS,), ((0, 8),), -0.2, 0.2), 6.0, 13.0)
    expert_ids_keys = jax.random.split(jax.random.fold_in(arg_keys[9], 1), SEQUENCE_TOKENS // SHARD_TOKENS)
    expert_ids_turns = jax.random.permutation(jax.random.fold_in(arg_keys[9], 3), SEQUENCE_TOKENS // SHARD_TOKENS)
    expert_ids = jax.vmap(lambda own, number: assign_block(jax.random.fold_in(arg_keys[9], 2), own, number, SHARD_TOKENS, EXPERTS, TOP, CAP, 2))(expert_ids_keys, expert_ids_turns).reshape((SEQUENCE_TOKENS, TOP))
    expert_weights = jnp.clip(0.1 + 0.5 * jax.random.uniform(arg_keys[10], (SEQUENCE_TOKENS, TOP), jnp.float32) ** block_scale(arg_keys[10], (SEQUENCE_TOKENS, TOP), ((0, 32),), -0.2, 0.2), 0.1, 0.6)
    w_gate = bell_draw(arg_keys[11], (EXPERTS, MODEL_WIDTH, FFE), MODEL_WIDTH ** -0.5, 0.109375, ((0, 32), (2, 8)))
    w_up = bell_draw(arg_keys[12], (EXPERTS, MODEL_WIDTH, FFE), MODEL_WIDTH ** -0.5, 0.109375, ((0, 32), (2, 8)))
    w_down = bell_draw(arg_keys[13], (EXPERTS, FFE, MODEL_WIDTH), FFE ** -0.5, 0.15625, ((0, 32), (1, 8)))
    return {"tokens": tokens, "positions": positions, "norm_attn": norm_attn, "norm_moe": norm_moe, "w_query": w_query, "key_matrix": key_matrix, "value_matrix": value_matrix, "w_out": w_out, "sinks": sinks, "expert_ids": expert_ids, "expert_weights": expert_weights, "w_gate": w_gate, "w_up": w_up, "w_down": w_down}


EPSILON = 1e-05

def rms_norm(values, gain_vector):
    mean_square = lax.optimization_barrier(jnp.mean(values * values, axis=-1, keepdims=True))
    return values * lax.rsqrt(mean_square + EPSILON) * gain_vector

def reference(tokens, positions, norm_attn, norm_moe, w_query, key_matrix, value_matrix, w_out, sinks, expert_ids, expert_weights, w_gate, w_up, w_down):
    group_width = QUERY_HEADS // KEY_VALUE_HEADS
    score_scale = HEAD_WIDTH ** (-0.5)
    hidden_in = tokens.astype(jnp.float32)
    normed = rms_norm(hidden_in, norm_attn).astype(jnp.bfloat16)
    query_rows = jnp.dot(normed, w_query, preferred_element_type=jnp.float32).astype(jnp.bfloat16)
    key_projected = jnp.dot(normed, key_matrix, preferred_element_type=jnp.float32).astype(jnp.bfloat16)
    value_projected = jnp.dot(normed, value_matrix, preferred_element_type=jnp.float32).astype(jnp.bfloat16)
    heads_of_keys = jnp.transpose(key_projected.reshape(SEQUENCE_TOKENS, KEY_VALUE_HEADS, HEAD_WIDTH), (1, 0, 2)).astype(jnp.float32)
    value_heads = jnp.transpose(value_projected.reshape(SEQUENCE_TOKENS, KEY_VALUE_HEADS, HEAD_WIDTH), (1, 0, 2)).astype(jnp.float32)
    blocks_of_queries = jnp.transpose(query_rows.reshape(SEQUENCE_TOKENS // SHARD_TOKENS, SHARD_TOKENS, KEY_VALUE_HEADS, group_width, HEAD_WIDTH), (0, 2, 1, 3, 4))
    block_positions = positions.reshape(SEQUENCE_TOKENS // SHARD_TOKENS, SHARD_TOKENS)
    sink_lattice = sinks.reshape(KEY_VALUE_HEADS, group_width)

    def one_block(block_args):
        block_query, block_pos = block_args
        visible = positions[None, None, :] <= block_pos[None, :, None]

        def one_head(head_args):
            head_query, head_keys, head_vals, head_sinks = head_args
            scores = jnp.einsum('qgd,kd->gqk', head_query.astype(jnp.float32), head_keys) * score_scale
            scores = jnp.where(visible, scores, -1e+30)
            top_row = jnp.maximum(lax.optimization_barrier(jnp.max(scores, axis=-1)), head_sinks[:, None])
            probs = jnp.exp(scores - top_row[..., None])
            denominator = lax.optimization_barrier(jnp.sum(probs, axis=-1)) + jnp.exp(head_sinks[:, None] - top_row)
            rounded = lax.optimization_barrier(probs.astype(jnp.bfloat16))
            mixed = jnp.einsum('gqk,kd->gqd', rounded.astype(jnp.float32), head_vals)
            return (mixed / denominator[..., None]).astype(jnp.bfloat16)
        per_head = lax.map(one_head, (block_query, heads_of_keys, value_heads, sink_lattice))
        return jnp.transpose(per_head, (2, 0, 1, 3)).reshape(SHARD_TOKENS, QUERY_HEADS * HEAD_WIDTH)
    head_out = lax.map(one_block, (blocks_of_queries, block_positions)).reshape(SEQUENCE_TOKENS, QUERY_HEADS * HEAD_WIDTH)
    attended = jnp.dot(head_out, w_out, preferred_element_type=jnp.float32).astype(jnp.bfloat16)
    residual = hidden_in + attended.astype(jnp.float32)
    moe_in = rms_norm(residual, norm_moe).astype(jnp.bfloat16)
    flat_ids = expert_ids.reshape(-1)
    flat_weights = expert_weights.reshape(-1)
    most_routes = SEQUENCE_TOKENS // SHARD_TOKENS * CAP
    group_units = FFE // N_EXP

    def one_expert(expert_sum, expert_args):
        expert_index, gate_w, up_w, down_w = expert_args
        chosen = flat_ids == expert_index
        order = jnp.argsort(jnp.where(chosen, 0, 1).astype(jnp.int32), stable=True)[:most_routes]
        taken = chosen[order]
        row_index = (order // TOP).astype(jnp.int32)
        inputs = moe_in[row_index]
        gate_act = jnp.dot(inputs, gate_w, preferred_element_type=jnp.float32)
        up_act = jnp.dot(inputs, up_w, preferred_element_type=jnp.float32)
        activated = (gate_act * jax.nn.sigmoid(1.702 * gate_act) * (up_act + 1.0)).astype(jnp.bfloat16)
        grouped = jnp.einsum('ngf,gfd->gnd', activated.reshape(most_routes, N_EXP, group_units).astype(jnp.float32), down_w.reshape(N_EXP, group_units, MODEL_WIDTH).astype(jnp.float32))
        rounded = lax.optimization_barrier(grouped.astype(jnp.bfloat16))
        expert_out = lax.optimization_barrier(jnp.sum(rounded.astype(jnp.float32), axis=0))
        route_weight = jnp.where(taken, flat_weights[order], jnp.float32(0.0))
        expert_sum = expert_sum.at[row_index].add(expert_out * route_weight[:, None])
        return (expert_sum, None)
    start_sum = jnp.zeros((SEQUENCE_TOKENS, MODEL_WIDTH), jnp.float32)
    expert_sum, _ = lax.scan(one_expert, start_sum, (jnp.arange(EXPERTS).astype(jnp.int32), w_gate, w_up, w_down))
    layer_out = (residual + expert_sum).astype(jnp.bfloat16)
    return (attended, layer_out)
```

```python
import functools

import jax
import jax.numpy as jnp
from jax import lax
from jax.experimental import pallas as pl
from jax.experimental.pallas import tpu as pltpu
from jax.sharding import PartitionSpec as P

HEAD_WIDTH = 64
EPSILON = 1e-05
CHUNK = 384
EXTRA = 16
BF16 = jnp.bfloat16
F32 = jnp.float32
VMEM = pl.BlockSpec(memory_space=pltpu.VMEM)
SMEM = pl.BlockSpec(memory_space=pltpu.SMEM)


def call(kernel, out_shapes, in_specs, vmem_mib=48):
    single = not isinstance(out_shapes, (list, tuple))
    out_specs = VMEM if single else [VMEM] * len(out_shapes)
    return pl.pallas_call(
        kernel,
        out_shape=out_shapes,
        in_specs=in_specs,
        out_specs=out_specs,
        compiler_params=pltpu.CompilerParams(vmem_limit_bytes=vmem_mib * 1024 * 1024),
    )


def shape(dims, dtype=BF16):
    return jax.ShapeDtypeStruct(dims, dtype)


def dot(a, b, contract=((1,), (0,))):
    return lax.dot_general(a, b, (contract, ((), ())), preferred_element_type=F32)


def spans(width):
    return [(start, min(CHUNK, width - start)) for start in range(0, width, CHUNK)]


def kv_kernel(pos_ref, tokens_ref, gain_ref, key_ref, value_ref, normed_ref, payload_ref):
    rows = tokens_ref.shape[0]
    values = tokens_ref[...].astype(F32)
    mean_square = jnp.mean(values * values, axis=-1, keepdims=True)
    normed = (values * lax.rsqrt(mean_square + EPSILON) * gain_ref[...]).astype(BF16)
    normed_ref[...] = normed
    keys = dot(normed, key_ref[...])
    vals = dot(normed, value_ref[...])
    payload_ref[:rows, :] = jnp.concatenate([keys, vals], axis=1).astype(BF16)
    base = pos_ref[0]
    lane = lax.broadcasted_iota(jnp.int32, (EXTRA, payload_ref.shape[1]), 1)
    marks = jnp.where(lane == 0, base // 128, jnp.where(lane == 1, base % 128, 0))
    payload_ref[rows:, :] = marks.astype(F32).astype(BF16)


def query_kernel(normed_ref, w_ref, out_ref):
    rows = normed_ref.shape[0]
    heads = w_ref.shape[1] // HEAD_WIDTH
    queries = dot(normed_ref[...], w_ref[...]).astype(BF16)
    queries = queries * jnp.asarray(HEAD_WIDTH ** (-0.5), BF16)
    for head in range(heads):
        out_ref[head * rows:(head + 1) * rows, :] = queries[
            :, head * HEAD_WIDTH:(head + 1) * HEAD_WIDTH
        ]


def route_kernel(experts, slots, ids_ref, weights_ref, gather_ref, combine_ref):
    rows, top = ids_ref.shape
    cells = experts * slots
    expert_lane = lax.broadcasted_iota(jnp.int32, (rows, experts), 1)
    chosen = [(ids_ref[:, k:k + 1] == expert_lane).astype(F32) for k in range(top)]
    named = functools.reduce(jnp.add, chosen)
    below = lax.broadcasted_iota(jnp.int32, (rows, rows), 1) < lax.broadcasted_iota(
        jnp.int32, (rows, rows), 0
    )
    place = dot(below.astype(BF16), named.astype(BF16)) + (expert_lane * slots).astype(F32)
    cell = lax.broadcasted_iota(jnp.int32, (rows, cells), 1).astype(F32)
    filled = jnp.zeros((rows, cells), F32)
    scaled = jnp.zeros((rows, cells), F32)
    for k in range(top):
        target = jnp.sum(chosen[k] * place, axis=1, keepdims=True)
        match = cell == target
        filled = jnp.where(match, 1.0, filled)
        scaled = jnp.where(match, weights_ref[:, k:k + 1], scaled)
    gather_ref[...] = filled.T.astype(BF16)
    for part in range(3):
        rounded = scaled.astype(BF16)
        combine_ref[part * rows:(part + 1) * rows, :] = rounded
        scaled = scaled - rounded.astype(F32)


def attention_kernel(blocks, pos_ref, query_ref, kv_ref, sink_ref, w_ref, out_ref):
    count, padded, pair = kv_ref.shape
    rows = padded - EXTRA
    columns = query_ref.shape[0]
    width = w_ref.shape[1]
    key_row = lax.broadcasted_iota(jnp.int32, (rows, columns), 0)
    query_row = lax.broadcasted_iota(jnp.int32, (rows, columns), 1) % rows
    offset = (key_row - query_row).astype(F32)
    mine = pos_ref[0].astype(F32)

    def step(turn, carry):
        top_old, den, mixed = carry
        parts = []
        held = []
        for j in range(blocks):
            block = turn * blocks + j
            marks = kv_ref[block, rows:rows + EXTRA, :].astype(F32)
            base = marks[0:1, 0:1] * 128.0 + marks[0:1, 1:2]
            kv = kv_ref[block, :rows, :]
            held.append(kv[:, HEAD_WIDTH:])
            scores = dot(kv[:, :HEAD_WIDTH], query_ref[...], ((1,), (1,)))
            parts.append(jnp.where(offset <= mine - base, scores, -1e30))
        scores = jnp.concatenate(parts, axis=0)
        vals = jnp.concatenate(held, axis=0)
        top_new = jnp.maximum(top_old, jnp.max(scores, axis=0, keepdims=True))
        rescale = jnp.exp(top_old - top_new)
        probs = jnp.exp(scores - top_new)
        den = den * rescale + jnp.sum(probs, axis=0, keepdims=True)
        mixed = mixed * rescale + dot(vals, probs.astype(BF16), ((0,), (0,)))
        return top_new, den, mixed

    start = (
        sink_ref[...],
        jnp.ones((1, columns), F32),
        jnp.zeros((pair - HEAD_WIDTH, columns), F32),
    )
    _, den, mixed = lax.fori_loop(0, count // blocks, step, start)
    heads = (mixed / den).astype(BF16)
    stacked = jnp.concatenate(
        [heads[:, head * rows:(head + 1) * rows] for head in range(columns // rows)], axis=0
    )
    for index, (first, size) in enumerate(spans(width)):
        part = dot(stacked, w_ref[:, first:first + size], ((0,), (0,))).astype(BF16)
        out_ref[index, :, :size] = part
        if size < CHUNK:
            out_ref[index, :, size:] = jnp.zeros((rows, CHUNK - size), BF16)


def residual_kernel(parts_ref, tokens_ref, attended_ref, residual_ref, squares_ref):
    total = parts_ref[0].astype(F32)
    for index in range(1, parts_ref.shape[0]):
        total = total + parts_ref[index].astype(F32)
    attended = total.astype(BF16)
    attended_ref[...] = attended
    residual = tokens_ref[...].astype(F32) + attended.astype(F32)
    residual_ref[...] = residual
    column = jnp.sum(residual * residual, axis=1, keepdims=True)
    squares_ref[...] = jnp.broadcast_to(column, (column.shape[0], 128)).T[:8, :]


def dispatch_kernel(width, squares_ref, residual_ref, gain_ref, gather_ref, out_ref):
    total = squares_ref[0]
    for index in range(1, squares_ref.shape[0]):
        total = total + squares_ref[index]
    column = jnp.broadcast_to(total[0:1, :], (total.shape[1], total.shape[1])).T[:, 0:1]
    scale = lax.rsqrt(column / width + EPSILON)
    moe_in = (residual_ref[...] * scale * gain_ref[...]).astype(BF16)
    out_ref[...] = dot(gather_ref[...], moe_in).astype(BF16)


def expert_kernel(width, sets, rows_ref, *refs):
    weights, out_ref = refs[:-1], refs[-1]
    hidden = []
    for index in range(sets):
        gate_ref, up_ref = weights[3 * index], weights[3 * index + 1]
        gate, up = 0.0, 0.0
        for place, (first, size) in enumerate(spans(width)):
            rows = rows_ref[place, :, :size]
            gate = gate + dot(rows, gate_ref[first:first + size, :])
            up = up + dot(rows, up_ref[first:first + size, :])
        hidden.append((gate * jax.nn.sigmoid(1.702 * gate) * (up + 1.0)).astype(BF16))
    for place, (first, size) in enumerate(spans(width)):
        part = 0.0
        for index in range(sets):
            part = part + dot(hidden[index], weights[3 * index + 2][:, first:first + size])
        out_ref[place, :, :size] = part.astype(BF16)
        if size < CHUNK:
            out_ref[place, :, size:] = jnp.zeros((part.shape[0], CHUNK - size), BF16)


def sum_kernel(groups, parts_ref, out_ref):
    for half, members in enumerate(groups):
        total = parts_ref[members[0]].astype(F32)
        for index in members[1:]:
            total = total + parts_ref[index].astype(F32)
        out_ref[half] = total.astype(BF16)


def combine_kernel(returned_ref, combine_ref, residual_ref, attended_ref, out_ref):
    rows = residual_ref.shape[0]
    mixed = dot(combine_ref[...], returned_ref[...])
    total = mixed[:rows] + mixed[rows:2 * rows] + mixed[2 * rows:]
    out_ref[:, :CHUNK] = attended_ref[...]
    out_ref[:, CHUNK:] = (residual_ref[...] + total).astype(BF16)


def finish_kernel(parts_ref, attended_ref, layer_ref):
    for index, (first, size) in enumerate(spans(attended_ref.shape[1])):
        attended_ref[:, first:first + size] = parts_ref[index, :, :size]
        layer_ref[:, first:first + size] = parts_ref[index, :, CHUNK:CHUNK + size]


def exchange(block, axis):
    return lax.all_to_all(block, axis, split_axis=0, concat_axis=0, tiled=True)


def local(
    tokens,
    positions,
    norm_attn,
    norm_moe,
    w_query,
    key_matrix,
    value_matrix,
    w_out,
    sinks,
    expert_ids,
    expert_weights,
    w_gate,
    w_up,
    w_down,
):
    ctx_count = lax.axis_size("ctx")
    exp_count = lax.axis_size("exp")
    rows, width = tokens.shape
    heads = sinks.shape[0]
    top = expert_ids.shape[1]
    experts = ctx_count
    slots = rows * top * 3 // (2 * experts)
    padded_width = exp_count * CHUNK
    member = lax.axis_index("exp")

    own = (w_gate[0], w_up[0], w_down[0])
    swap = [(i, i ^ 2) for i in range(exp_count)]
    other = tuple(lax.ppermute(w, "exp", swap) for w in own)

    normed, payload = call(
        kv_kernel,
        [shape((rows, width)), shape((rows + EXTRA, 2 * HEAD_WIDTH))],
        [SMEM, VMEM, VMEM, VMEM, VMEM],
    )(positions, tokens, norm_attn[None], key_matrix, value_matrix)
    gathered = exchange(jnp.broadcast_to(payload[None], (ctx_count,) + payload.shape), "ctx")
    queries = call(query_kernel, shape((heads * rows, HEAD_WIDTH)), [VMEM, VMEM])(normed, w_query)
    gather_table, combine_table = call(
        functools.partial(route_kernel, experts, slots),
        [shape((experts * slots, rows)), shape((3 * rows, experts * slots))],
        [VMEM, VMEM],
    )(expert_ids, expert_weights)
    sink_row = jnp.repeat(sinks, rows)[None]
    own_tokens = lax.dynamic_slice_in_dim(
        jnp.pad(tokens, ((0, 0), (0, padded_width - width))), member * CHUNK, CHUNK, 1
    )
    own_gain = lax.dynamic_slice_in_dim(
        jnp.pad(norm_moe, (0, padded_width - width)), member * CHUNK, CHUNK, 0
    )[None]

    partial_sums = call(
        functools.partial(attention_kernel, 4),
        shape((exp_count, rows, CHUNK)),
        [SMEM, VMEM, VMEM, VMEM, VMEM],
    )(positions, queries, gathered, sink_row, w_out)
    parts = exchange(partial_sums, "exp")
    attended, residual, squares = call(
        residual_kernel,
        [shape((rows, CHUNK)), shape((rows, CHUNK), F32), shape((8, rows), F32)],
        [VMEM, VMEM],
    )(parts, own_tokens)
    all_squares = exchange(jnp.broadcast_to(squares[None], (exp_count, 8, rows)), "exp")
    outgoing = call(
        functools.partial(dispatch_kernel, width),
        shape((experts * slots, CHUNK)),
        [VMEM, VMEM, VMEM, VMEM],
    )(all_squares, residual, own_gain, gather_table)

    arrived = exchange(outgoing.reshape(ctx_count, slots, CHUNK), "ctx")
    halves = arrived.reshape(2, ctx_count * slots // 2, CHUNK)
    expert_rows = exchange(
        jnp.stack([halves[(i >> 1) & 1] for i in range(exp_count)]), "exp"
    )
    products = call(
        functools.partial(expert_kernel, width, 2),
        shape(expert_rows.shape),
        [VMEM] * 7,
        56,
    )(expert_rows, *own, *other)
    product_parts = exchange(products, "exp")
    groups = [[i for i in range(exp_count) if (i >> 1) & 1 == half] for half in range(2)]
    summed = call(functools.partial(sum_kernel, groups), shape(halves.shape), [VMEM])(product_parts)
    returned = exchange(summed.reshape(ctx_count, slots, CHUNK), "ctx")
    final = call(combine_kernel, shape((rows, 2 * CHUNK)), [VMEM] * 4)(
        returned.reshape(experts * slots, CHUNK), combine_table, residual, attended
    )
    final = exchange(final.reshape(exp_count, rows // exp_count, 2 * CHUNK), "exp")
    out = shape((rows // exp_count, width))
    return tuple(call(finish_kernel, [out, out], [VMEM])(final))


def solution(mesh):
    in_specs = (
        P("ctx", None),
        P("ctx"),
        P(),
        P(),
        P(None, "exp"),
        P(None, "exp"),
        P(None, "exp"),
        P("exp", None),
        P("exp"),
        P("ctx", None),
        P("ctx", None),
        P("ctx", None, "exp"),
        P("ctx", None, "exp"),
        P("ctx", "exp", None),
    )
    out_specs = (P(("ctx", "exp"), None), P(("ctx", "exp"), None))
    return jax.shard_map(local, mesh=mesh, in_specs=in_specs, out_specs=out_specs, check_vma=False)
```

```python
import functools

import jax
import jax.numpy as jnp
from jax import lax
from jax.experimental import pallas as pl
from jax.experimental.pallas import tpu as pltpu
from jax.sharding import PartitionSpec as P

HEAD_WIDTH = 64
EPSILON = 1e-05
CHUNK = 384
TAIL = 16
MAIN = CHUNK - TAIL
EXTRA = 16
BF16 = jnp.bfloat16
F32 = jnp.float32
VMEM = pl.BlockSpec(memory_space=pltpu.VMEM)
SMEM = pl.BlockSpec(memory_space=pltpu.SMEM)
HBM = pl.BlockSpec(memory_space=pltpu.HBM)


def in_hbm(array):
    return pltpu.with_memory_space_constraint(array, pltpu.HBM)


def call(kernel, out_shapes, in_specs, vmem_mib=24):
    single = not isinstance(out_shapes, (list, tuple))
    out_specs = VMEM if single else [VMEM] * len(out_shapes)
    return pl.pallas_call(
        kernel,
        out_shape=out_shapes,
        in_specs=in_specs,
        out_specs=out_specs,
        compiler_params=pltpu.CompilerParams(vmem_limit_bytes=vmem_mib * 1024 * 1024),
    )


def shape(dims, dtype=BF16):
    return jax.ShapeDtypeStruct(dims, dtype)


def dot(a, b, contract=((1,), (0,))):
    return lax.dot_general(a, b, (contract, ((), ())), preferred_element_type=F32)


def spans(width):
    return [(start, min(CHUNK, width - start)) for start in range(0, width, CHUNK)]


def fetch(sources, held, sems):
    copies = [
        pltpu.make_async_copy(source, target, sems.at[index])
        for index, (source, target) in enumerate(zip(sources, held))
    ]
    for copy in copies:
        copy.start()
    return copies


def tail_spans(width):
    full = width // CHUNK
    return [(full * CHUNK, width - full * CHUNK)] + [
        (place * CHUNK + MAIN, TAIL) for place in range(full)
    ]


def kv_kernel(
    pos_ref, tokens_hbm, gain_hbm, key_hbm, value_hbm, normed_ref, payload_ref,
    tokens_ref, gain_ref, key_ref, value_ref, sems,
):
    sources = (tokens_hbm, gain_hbm, key_hbm, value_hbm)
    copies = fetch(sources, (tokens_ref, gain_ref, key_ref, value_ref), sems)
    rows = tokens_ref.shape[1]
    copies[0].wait()
    values = tokens_ref[...].T.astype(F32)
    mean_square = jnp.mean(values * values, axis=-1, keepdims=True)
    copies[1].wait()
    normed = (values * lax.rsqrt(mean_square + EPSILON) * gain_ref[...][None, :]).astype(BF16)
    normed_ref[...] = normed
    copies[2].wait()
    keys = dot(normed, key_ref[...], ((1,), (1,)))
    copies[3].wait()
    vals = dot(normed, value_ref[...], ((1,), (1,)))
    payload_ref[:rows, :] = jnp.concatenate([keys, vals], axis=1).astype(BF16)
    base = pos_ref[0]
    lane = lax.broadcasted_iota(jnp.int32, (EXTRA, payload_ref.shape[1]), 1)
    marks = jnp.where(lane == 0, base // 128, jnp.where(lane == 1, base % 128, 0))
    payload_ref[rows:, :] = marks.astype(F32).astype(BF16)


def project_kv(positions, tokens, gain, keys, vals):
    width, rows = tokens.shape
    arrays = (tokens, gain, keys, vals)
    return pl.pallas_call(
        kv_kernel,
        out_shape=[shape((rows, width)), shape((rows + EXTRA, 2 * HEAD_WIDTH))],
        in_specs=[SMEM] + [HBM] * 4,
        out_specs=[VMEM, VMEM],
        scratch_shapes=[pltpu.VMEM(a.shape, a.dtype) for a in arrays]
        + [pltpu.SemaphoreType.DMA((4,))],
        compiler_params=pltpu.CompilerParams(vmem_limit_bytes=32 * 1024 * 1024),
    )(in_hbm(positions), *[in_hbm(a) for a in arrays])


def query_kernel(normed_ref, w_ref, out_ref):
    rows = normed_ref.shape[0]
    heads = w_ref.shape[1] // HEAD_WIDTH
    queries = dot(normed_ref[...], w_ref[...]).astype(BF16)
    queries = queries * jnp.asarray(HEAD_WIDTH ** (-0.5), BF16)
    lane = lax.broadcasted_iota(jnp.int32, (rows, HEAD_WIDTH), 1)
    flag = jnp.where(lane == 0, 1.0, 0.0).astype(BF16)
    for head in range(heads):
        own = queries[:, head * HEAD_WIDTH:(head + 1) * HEAD_WIDTH]
        out_ref[head * rows:(head + 1) * rows, :] = jnp.concatenate([own, flag], axis=1)


def upright(ref):
    spare = jnp.zeros((8 - ref.shape[0], ref.shape[1]), F32)
    return jnp.concatenate([ref[...].astype(F32), spare], axis=0).T


def prepare_kernel(
    experts, slots, member_ref, ids_ref, weights_ref, tokens_ref, gain_ref,
    gather_ref, combine_ref, own_tokens_ref, own_gain_ref, gain_scratch,
):
    top, rows = ids_ref.shape
    cells = experts * slots
    ids, weights = upright(ids_ref), upright(weights_ref)
    expert_lane = lax.broadcasted_iota(jnp.int32, (rows, experts), 1).astype(F32)
    chosen = [(ids[:, k:k + 1] == expert_lane).astype(F32) for k in range(top)]
    named = functools.reduce(jnp.add, chosen)
    below = lax.broadcasted_iota(jnp.int32, (rows, rows), 1) < lax.broadcasted_iota(
        jnp.int32, (rows, rows), 0
    )
    place = dot(below.astype(BF16), named.astype(BF16)) + expert_lane * slots
    cell = lax.broadcasted_iota(jnp.int32, (rows, cells), 1).astype(F32)
    filled = jnp.zeros((rows, cells), F32)
    scaled = jnp.zeros((rows, cells), F32)
    for k in range(top):
        target = jnp.sum(chosen[k] * place, axis=1, keepdims=True)
        match = cell == target
        filled = jnp.where(match, 1.0, filled)
        scaled = jnp.where(match, weights[:, k:k + 1], scaled)
    gather_ref[...] = filled.T.astype(BF16)
    for part in range(3):
        rounded = scaled.astype(BF16)
        combine_ref[part * rows:(part + 1) * rows, :] = rounded
        scaled = scaled - rounded.astype(F32)

    width = tokens_ref.shape[0]
    full = width // CHUNK
    rest = width - full * CHUNK
    tails = tail_spans(width)
    spare = CHUNK - sum(size for _, size in tails)
    member = member_ref[0]
    is_last = jnp.full((1, 1), member, jnp.int32) == full
    start = pl.multiple_of(member * CHUNK, rest)
    second = pl.multiple_of(jnp.minimum(start + CHUNK - rest, full * CHUNK), rest)
    main = jnp.concatenate(
        [tokens_ref[pl.ds(start, rest), :], tokens_ref[pl.ds(second, CHUNK - rest), :]], axis=0
    ).astype(F32)
    tail = jnp.concatenate(
        [tokens_ref[first:first + size, :].astype(F32) for first, size in tails]
        + [jnp.zeros((spare, rows), F32)],
        axis=0,
    )
    feature = lax.broadcasted_iota(jnp.int32, main.shape, 0)
    own = jnp.where(is_last, tail, jnp.where(feature < MAIN, main, 0.0))
    own_tokens_ref[...] = own.T.astype(BF16)

    gain = gain_ref[...][None, :]
    gain_scratch[:, :width] = gain
    gain_scratch[:, width:] = jnp.zeros((1, gain_scratch.shape[1] - width), F32)
    main = gain_scratch[:, pl.ds(pl.multiple_of(member * CHUNK, 128), CHUNK)]
    tail = jnp.concatenate(
        [gain[:, first:first + size] for first, size in tails] + [jnp.zeros((1, spare), F32)], axis=1
    )
    feature = lax.broadcasted_iota(jnp.int32, main.shape, 1)
    own_gain_ref[...] = jnp.where(is_last, tail, jnp.where(feature < MAIN, main, 0.0))


def prepare(experts, slots, member, ids, weights, tokens, gain):
    width, rows = tokens.shape
    return pl.pallas_call(
        functools.partial(prepare_kernel, experts, slots),
        out_shape=[
            shape((experts * slots, rows)),
            shape((3 * rows, experts * slots)),
            shape((rows, CHUNK)),
            shape((1, CHUNK), F32),
        ],
        in_specs=[SMEM] + [VMEM] * 4,
        out_specs=[VMEM] * 4,
        scratch_shapes=[pltpu.VMEM((1, (width // CHUNK + 1) * CHUNK), F32)],
        compiler_params=pltpu.CompilerParams(vmem_limit_bytes=24 * 1024 * 1024),
    )(member.reshape(1), ids, weights, tokens, gain)


def attend(pos_ref, query_ref, kv_refs, carry, diagonal=False):
    rows = kv_refs[0].shape[1] - EXTRA
    mine = pos_ref[0].astype(F32)
    key_side = lax.broadcasted_iota(jnp.int32, (rows, 2 * HEAD_WIDTH), 1) < HEAD_WIDTH
    flag_lane = lax.broadcasted_iota(jnp.int32, (rows, 2 * HEAD_WIDTH), 1) == HEAD_WIDTH
    top, mixed = carry
    for _ in range(1):
        keys = []
        vals = []
        for kv_ref, block in [(ref, i) for ref in kv_refs for i in range(ref.shape[0])]:
            marks = kv_ref[block, rows:rows + EXTRA, :].astype(F32)
            base = marks[0:1, 0:1] * 128.0 + marks[0:1, 1:2]
            hidden = jnp.where(base <= mine, 0.0, -1e30)
            kv = kv_ref[block, :rows, :].astype(F32)
            keys.append(jnp.where(key_side, kv, jnp.where(flag_lane, hidden, 0.0)).astype(BF16))
            vals.append(jnp.where(key_side, 1.0, kv).astype(BF16))
        keys = jnp.concatenate(keys, axis=0)
        vals = jnp.concatenate(vals, axis=0)
        scores = dot(query_ref[...], keys, ((1,), (1,)))
        if diagonal:
            own = scores[:, :rows]
            query_row = lax.broadcasted_iota(jnp.int32, own.shape, 0) % rows
            key_row = lax.broadcasted_iota(jnp.int32, own.shape, 1)
            own = jnp.where(key_row <= query_row, own, -1e30)
            scores = jnp.concatenate([own, scores[:, rows:]], axis=1)
        top_new = jnp.maximum(top, jnp.max(scores, axis=1, keepdims=True))
        probs = jnp.exp(scores - top_new).astype(BF16)
        mixed = mixed * jnp.exp(top - top_new) + dot(probs, vals)
        top = top_new
    return top, mixed


def first_attention_kernel(pos_ref, sink_ref, query_ref, *refs):
    *kv_refs, top_ref, mixed_ref = refs
    columns = query_ref.shape[0]
    heads = sink_ref.shape[0]
    top = jnp.concatenate(
        [jnp.full((columns // heads, 1), sink_ref[head], F32) for head in range(heads)], axis=0
    )
    lane = lax.broadcasted_iota(jnp.int32, (columns, 2 * HEAD_WIDTH), 1)
    start = (top, jnp.where(lane < HEAD_WIDTH, 1.0, 0.0))
    top_ref[...], mixed_ref[...] = attend(pos_ref, query_ref, kv_refs, start, True)


def middle_attention_kernel(pos_ref, query_ref, old_top_ref, old_mixed_ref, *refs):
    *kv_refs, top_ref, mixed_ref = refs
    carry = (old_top_ref[...], old_mixed_ref[...])
    top_ref[...], mixed_ref[...] = attend(pos_ref, query_ref, kv_refs, carry)


def last_attention_kernel(pos_ref, query_ref, old_top_ref, old_mixed_ref, w_ref, *refs):
    *kv_refs, out_ref = refs
    width = w_ref.shape[0]
    columns = query_ref.shape[0]
    rows = out_ref.shape[1]
    _, mixed = attend(pos_ref, query_ref, kv_refs, (old_top_ref[...], old_mixed_ref[...]))
    heads = (mixed[:, HEAD_WIDTH:] / mixed[:, :HEAD_WIDTH]).astype(BF16)
    stacked = jnp.concatenate(
        [heads[head * rows:(head + 1) * rows] for head in range(columns // rows)], axis=1
    )
    full = width // CHUNK
    for place in range(full):
        part = dot(stacked, w_ref[place * CHUNK:(place + 1) * CHUNK, :], ((1,), (1,)))
        out_ref[place] = part.astype(BF16)
    tail = jnp.concatenate(
        [w_ref[first:first + size, :] for first, size in tail_spans(width)], axis=0
    )
    out_ref[full] = jnp.zeros((rows, CHUNK), BF16)
    out_ref[full, :, :tail.shape[0]] = dot(stacked, tail, ((1,), (1,))).astype(BF16)


def dispatch_kernel(
    parts_ref, tokens_ref, gain_ref, gather_ref, attended_ref, residual_ref, out_ref
):
    total = parts_ref[0].astype(F32)
    for index in range(1, parts_ref.shape[0]):
        total = total + parts_ref[index].astype(F32)
    lane = lax.broadcasted_iota(jnp.int32, total.shape, 1)
    attended = jnp.where(lane < MAIN, total, 0.0).astype(BF16)
    attended_ref[...] = attended
    residual = tokens_ref[...].astype(F32) + attended.astype(F32)
    residual_ref[...] = residual
    left = jnp.sum(residual * residual, axis=1, keepdims=True)
    moe_in = residual * gain_ref[...]
    for place in range(3):
        rounded = left.astype(BF16).astype(F32)
        moe_in = jnp.where(lane == MAIN + place, rounded, moe_in)
        left = left - rounded
    out_ref[...] = dot(gather_ref[...], moe_in.astype(BF16)).astype(BF16)


def expert_kernel(width, counts, rows_in_ref, *refs):
    *weights, out_ref, rows_ref = refs
    full = width // CHUNK
    split = CHUNK - 128
    count = rows_in_ref.shape[1]
    main_lane = lax.broadcasted_iota(jnp.int32, (count, 128), 1) < MAIN - split
    squares = jnp.zeros((count, 128), F32)
    for place in range(full + 1):
        last = rows_in_ref[place, :, split:].astype(F32)
        squares = squares + jnp.where(main_lane, 0.0, last)
        if place < full:
            first = place * CHUNK
            rows_ref[:, first:first + split] = rows_in_ref[place, :, :split]
            rows_ref[:, first + split:first + CHUNK] = jnp.where(main_lane, last, 0.0).astype(BF16)
    squares = jnp.sum(squares, axis=1, keepdims=True)
    scale = lax.rsqrt(squares / width + EPSILON)
    tails = tail_spans(width)
    tail_width = sum(size for _, size in tails)
    tail_rows = rows_in_ref[full, :, :tail_width]

    def columns(refs_in, first, size):
        start = 0
        for ref in refs_in:
            if start <= first < start + ref.shape[1]:
                return ref[:, first - start:first - start + size]
            start += ref.shape[1]

    def tail(refs_in):
        return jnp.concatenate([columns(refs_in, *span) for span in tails], axis=1)

    def product(ref):
        main = dot(rows_ref[...], ref[:, :full * CHUNK], ((1,), (1,)))
        return (main + dot(tail_rows, tail([ref]), ((1,), (1,)))) * scale

    hidden = []
    downs = []
    at = 0
    for number in counts:
        gate = product(weights[at])
        up = product(weights[at + 1])
        hidden.append((gate * jax.nn.sigmoid(1.702 * gate) * (up + 1.0)).astype(BF16))
        downs.append(weights[at + 2:at + number])
        at += number
    for place in range(full):
        part = 0.0
        for act, down in zip(hidden, downs):
            part = part + dot(act, columns(down, place * CHUNK, CHUNK))
        out_ref[place] = part.astype(BF16)
    part = 0.0
    for act, down in zip(hidden, downs):
        part = part + dot(act, tail(down))
    out_ref[full] = jnp.zeros(out_ref.shape[1:], BF16)
    out_ref[full, :, :tail_width] = part.astype(BF16)


def run_experts(width, expert_rows, sets):
    weights = [w for one in sets for w in one]
    count, rows, _ = expert_rows.shape
    return pl.pallas_call(
        functools.partial(expert_kernel, width, [len(one) for one in sets]),
        out_shape=shape(expert_rows.shape),
        in_specs=[VMEM] * (1 + len(weights)),
        out_specs=VMEM,
        scratch_shapes=[pltpu.VMEM((rows, width // CHUNK * CHUNK), BF16)],
        compiler_params=pltpu.CompilerParams(vmem_limit_bytes=24 * 1024 * 1024),
    )(expert_rows, *weights)


def sum_kernel(groups, parts_ref, out_ref):
    for half, members in enumerate(groups):
        total = parts_ref[members[0]].astype(F32)
        for index in members[1:]:
            total = total + parts_ref[index].astype(F32)
        out_ref[half] = total.astype(BF16)


def combine_kernel(returned_ref, combine_ref, residual_ref, attended_ref, out_ref):
    rows = residual_ref.shape[0]
    mixed = dot(combine_ref[...], returned_ref[...])
    total = mixed[:rows] + mixed[rows:2 * rows] + mixed[2 * rows:]
    out_ref[:, :CHUNK] = attended_ref[...]
    out_ref[:, CHUNK:] = (residual_ref[...] + total).astype(BF16)


def finish_kernel(parts_ref, attended_ref, layer_ref):
    width = attended_ref.shape[1]
    full = width // CHUNK
    for out_ref, at in ((attended_ref, 0), (layer_ref, CHUNK)):
        last = parts_ref[full, :, at:at + CHUNK].astype(F32)
        rest = width - full * CHUNK
        for place in range(full):
            start = rest + place * TAIL
            main = parts_ref[place, :, at:at + MAIN].astype(F32)
            whole = jnp.concatenate([main, last[:, start:start + TAIL]], axis=1)
            out_ref[:, place * CHUNK:(place + 1) * CHUNK] = whole.astype(BF16)
        out_ref[:, full * CHUNK:] = last[:, :rest].astype(BF16)


def exchange(block, axis, groups=None):
    return lax.all_to_all(
        block, axis, split_axis=0, concat_axis=0, tiled=True, axis_index_groups=groups
    )


def local(
    tokens,
    positions,
    norm_attn,
    norm_moe,
    w_query,
    key_matrix,
    value_matrix,
    w_out,
    sinks,
    expert_ids,
    expert_weights,
    w_gate,
    w_up,
    w_down,
):
    ctx_count = lax.axis_size("ctx")
    exp_count = lax.axis_size("exp")
    rows, width = tokens.shape
    heads = sinks.shape[0]
    top = expert_ids.shape[1]
    experts = ctx_count
    slots = rows * top * 3 // (2 * experts)
    member = lax.axis_index("exp")

    swap = [(i, i ^ 2) for i in range(exp_count)]
    gate, up, down = w_gate[0].T, w_up[0].T, w_down[0]

    normed, payload = project_kv(
        positions, tokens.T, norm_attn, key_matrix.T, value_matrix.T
    )
    far_gate = lax.ppermute(gate, "exp", swap)

    def moved(block, x, z, core):
        route = []
        for i in range(ctx_count):
            there = (i // 8 + x) % 4 * 8 + (i // 2 % 4 + z) % 4 * 2 + (i % 2 + core) % 2
            route.append((i, there))
        return lax.ppermute(block, "ctx", route)

    queries = call(query_kernel, shape((heads * rows, 2 * HEAD_WIDTH)), [VMEM, VMEM])(normed, w_query)
    stops = [moved(payload, 0, z, 0) for z in range(1, 4)]
    *stops, queries = lax.optimization_barrier((*stops, queries))
    column = jnp.stack([payload] + stops)
    column_far = moved(column, 0, 0, 1)
    planes = [moved(column, x, 0, 0) for x in range(1, 4)]
    state = [shape((heads * rows, 1), F32), shape((heads * rows, 2 * HEAD_WIDTH), F32)]
    carried = call(first_attention_kernel, state, [SMEM, SMEM] + [VMEM] * 3)(
        positions, sinks, queries, column, column_far
    )
    prepared = prepare(
        experts, slots, member, expert_ids.T, expert_weights.T, tokens.T, norm_moe
    )
    *planes, top_row, mixed, gather_table, combine_table, own_tokens, own_gain = (
        lax.optimization_barrier((*planes, *carried, *prepared))
    )
    planes_far = [moved(plane, 0, 0, 1) for plane in planes]
    carried = call(middle_attention_kernel, state, [SMEM] + [VMEM] * 6)(
        positions, queries, top_row, mixed, *planes
    )
    top_row, mixed, far_gate = lax.optimization_barrier((*carried, far_gate))
    far_up = lax.ppermute(up, "exp", swap)
    partial_sums = call(
        last_attention_kernel, shape((exp_count, rows, CHUNK)), [SMEM] + [VMEM] * 7
    )(positions, queries, top_row, mixed, w_out.T, *planes_far)
    partial_sums, far_up = lax.optimization_barrier((partial_sums, far_up))
    parts = exchange(partial_sums, "exp")
    parts, down = lax.optimization_barrier((parts, down))
    attended, residual, outgoing = call(
        dispatch_kernel,
        [shape((rows, CHUNK)), shape((rows, CHUNK), F32), shape((experts * slots, CHUNK))],
        [VMEM] * 4,
    )(parts, own_tokens, own_gain, gather_table)
    arrived = exchange(outgoing.reshape(ctx_count, slots, CHUNK), "ctx")
    far_down = lax.ppermute(down, "exp", swap)
    arrived, far_down = lax.optimization_barrier((arrived, far_down))
    halves = arrived.reshape(1, 2, 1, ctx_count * slots // 2, CHUNK)
    spread = jnp.broadcast_to(halves, (exp_count // 4, 2, 2) + halves.shape[3:])
    expert_rows = exchange(spread.reshape((exp_count,) + halves.shape[3:]), "exp")
    sets = [(gate, up, down), (far_gate, far_up, far_down)]
    products = run_experts(width, expert_rows, sets)
    product_parts = exchange(products, "exp")
    groups = [[i for i in range(exp_count) if (i >> 1) & 1 == half] for half in range(2)]
    summed = call(
        functools.partial(sum_kernel, groups),
        shape((2, ctx_count * slots // 2, CHUNK)),
        [VMEM],
    )(product_parts)
    returned = exchange(summed.reshape(ctx_count, slots, CHUNK), "ctx")
    final = call(combine_kernel, shape((rows, 2 * CHUNK)), [VMEM] * 4)(
        returned.reshape(experts * slots, CHUNK), combine_table, residual, attended
    )
    final = exchange(final.reshape(exp_count, rows // exp_count, 2 * CHUNK), "exp")
    out = shape((rows // exp_count, width))
    return tuple(call(finish_kernel, [out, out], [VMEM])(final))


def solution(mesh):
    in_specs = (
        P("ctx", None),
        P("ctx"),
        P(),
        P(),
        P(None, "exp"),
        P(None, "exp"),
        P(None, "exp"),
        P("exp", None),
        P("exp"),
        P("ctx", None),
        P("ctx", None),
        P("ctx", None, "exp"),
        P("ctx", None, "exp"),
        P("ctx", "exp", None),
    )
    out_specs = (P(("ctx", "exp"), None), P(("ctx", "exp"), None))
    return jax.shard_map(local, mesh=mesh, in_specs=in_specs, out_specs=out_specs, check_vma=False)
```

```python
import functools

import jax
import jax.numpy as jnp
from jax import lax
from jax.experimental import pallas as pl
from jax.experimental.pallas import tpu as pltpu
from jax.sharding import PartitionSpec as P

HEAD_WIDTH = 64
EPSILON = 1e-05
CHUNK = 384
TAIL = 16
LATE = 64
MAIN = CHUNK - TAIL
EXTRA = 16
BF16 = jnp.bfloat16
F32 = jnp.float32
VMEM = pl.BlockSpec(memory_space=pltpu.VMEM)
SMEM = pl.BlockSpec(memory_space=pltpu.SMEM)
HBM = pl.BlockSpec(memory_space=pltpu.HBM)


def in_hbm(array):
    return pltpu.with_memory_space_constraint(array, pltpu.HBM)


def call(kernel, out_shapes, in_specs, vmem_mib=24):
    single = not isinstance(out_shapes, (list, tuple))
    out_specs = VMEM if single else [VMEM] * len(out_shapes)
    return pl.pallas_call(
        kernel,
        out_shape=out_shapes,
        in_specs=in_specs,
        out_specs=out_specs,
        compiler_params=pltpu.CompilerParams(vmem_limit_bytes=vmem_mib * 1024 * 1024),
    )


def shape(dims, dtype=BF16):
    return jax.ShapeDtypeStruct(dims, dtype)


def dot(a, b, contract=((1,), (0,))):
    return lax.dot_general(a, b, (contract, ((), ())), preferred_element_type=F32)


def spans(width):
    return [(start, min(CHUNK, width - start)) for start in range(0, width, CHUNK)]


def fetch(sources, held, sems):
    copies = [
        pltpu.make_async_copy(source, target, sems.at[index])
        for index, (source, target) in enumerate(zip(sources, held))
    ]
    for copy in copies:
        copy.start()
    return copies


def tail_spans(width):
    full = width // CHUNK
    return [(full * CHUNK, width - full * CHUNK)] + [
        (place * CHUNK + MAIN, TAIL) for place in range(full)
    ]


def kv_kernel(
    pos_ref, tokens_hbm, gain_hbm, key_hbm, value_hbm, normed_ref, payload_ref,
    tokens_ref, gain_ref, key_ref, value_ref, sems,
):
    sources = (tokens_hbm, gain_hbm, key_hbm, value_hbm)
    copies = fetch(sources, (tokens_ref, gain_ref, key_ref, value_ref), sems)
    rows = tokens_ref.shape[1]
    copies[0].wait()
    values = tokens_ref[...].T.astype(F32)
    mean_square = jnp.mean(values * values, axis=-1, keepdims=True)
    copies[1].wait()
    normed = (values * lax.rsqrt(mean_square + EPSILON) * gain_ref[...][None, :]).astype(BF16)
    normed_ref[...] = normed
    copies[2].wait()
    keys = dot(normed, key_ref[...], ((1,), (1,)))
    copies[3].wait()
    vals = dot(normed, value_ref[...], ((1,), (1,)))
    payload_ref[:rows, :] = jnp.concatenate([keys, vals], axis=1).astype(BF16)
    base = pos_ref[0]
    lane = lax.broadcasted_iota(jnp.int32, (EXTRA, payload_ref.shape[1]), 1)
    marks = jnp.where(lane == 0, base // 128, jnp.where(lane == 1, base % 128, 0))
    payload_ref[rows:, :] = marks.astype(F32).astype(BF16)


def project_kv(positions, tokens, gain, keys, vals):
    width, rows = tokens.shape
    arrays = (tokens, gain, keys, vals)
    return pl.pallas_call(
        kv_kernel,
        out_shape=[shape((rows, width)), shape((rows + EXTRA, 2 * HEAD_WIDTH))],
        in_specs=[SMEM] + [HBM] * 4,
        out_specs=[VMEM, VMEM],
        scratch_shapes=[pltpu.VMEM(a.shape, a.dtype) for a in arrays]
        + [pltpu.SemaphoreType.DMA((4,))],
        compiler_params=pltpu.CompilerParams(vmem_limit_bytes=32 * 1024 * 1024),
    )(in_hbm(positions), *[in_hbm(a) for a in arrays])


def query_kernel(normed_ref, w_ref, out_ref):
    rows = normed_ref.shape[0]
    heads = w_ref.shape[1] // HEAD_WIDTH
    queries = dot(normed_ref[...], w_ref[...]).astype(BF16)
    queries = queries * jnp.asarray(HEAD_WIDTH ** (-0.5), BF16)
    lane = lax.broadcasted_iota(jnp.int32, (rows, HEAD_WIDTH), 1)
    flag = jnp.where(lane == 0, 1.0, 0.0).astype(BF16)
    for head in range(heads):
        own = queries[:, head * HEAD_WIDTH:(head + 1) * HEAD_WIDTH]
        out_ref[head * rows:(head + 1) * rows, :] = jnp.concatenate([own, flag], axis=1)


def upright(ref):
    spare = jnp.zeros((8 - ref.shape[0], ref.shape[1]), F32)
    return jnp.concatenate([ref[...].astype(F32), spare], axis=0).T


def prepare_kernel(
    experts, slots, member_ref, ids_ref, weights_ref, tokens_ref, gain_ref,
    gather_ref, combine_ref, own_tokens_ref, own_gain_ref, gain_scratch,
):
    top, rows = ids_ref.shape
    cells = experts * slots
    ids, weights = upright(ids_ref), upright(weights_ref)
    expert_lane = lax.broadcasted_iota(jnp.int32, (rows, experts), 1).astype(F32)
    chosen = [(ids[:, k:k + 1] == expert_lane).astype(F32) for k in range(top)]
    named = functools.reduce(jnp.add, chosen)
    below = lax.broadcasted_iota(jnp.int32, (rows, rows), 1) < lax.broadcasted_iota(
        jnp.int32, (rows, rows), 0
    )
    place = dot(below.astype(BF16), named.astype(BF16)) + expert_lane * slots
    cell = lax.broadcasted_iota(jnp.int32, (rows, cells), 1).astype(F32)
    filled = jnp.zeros((rows, cells), F32)
    scaled = jnp.zeros((rows, cells), F32)
    for k in range(top):
        target = jnp.sum(chosen[k] * place, axis=1, keepdims=True)
        match = cell == target
        filled = jnp.where(match, 1.0, filled)
        scaled = jnp.where(match, weights[:, k:k + 1], scaled)
    gather_ref[...] = filled.T.astype(BF16)
    for part in range(3):
        rounded = scaled.astype(BF16)
        combine_ref[part * rows:(part + 1) * rows, :] = rounded
        scaled = scaled - rounded.astype(F32)

    width = tokens_ref.shape[0]
    full = width // CHUNK
    rest = width - full * CHUNK
    tails = tail_spans(width)
    spare = CHUNK - sum(size for _, size in tails)
    member = member_ref[0]
    is_last = jnp.full((1, 1), member, jnp.int32) == full
    start = pl.multiple_of(member * CHUNK, rest)
    second = pl.multiple_of(jnp.minimum(start + CHUNK - rest, full * CHUNK), rest)
    main = jnp.concatenate(
        [tokens_ref[pl.ds(start, rest), :], tokens_ref[pl.ds(second, CHUNK - rest), :]], axis=0
    ).astype(F32)
    tail = jnp.concatenate(
        [tokens_ref[first:first + size, :].astype(F32) for first, size in tails]
        + [jnp.zeros((spare, rows), F32)],
        axis=0,
    )
    feature = lax.broadcasted_iota(jnp.int32, main.shape, 0)
    own = jnp.where(is_last, tail, jnp.where(feature < MAIN, main, 0.0))
    own_tokens_ref[...] = own.T.astype(BF16)

    gain = gain_ref[...][None, :]
    gain_scratch[:, :width] = gain
    gain_scratch[:, width:] = jnp.zeros((1, gain_scratch.shape[1] - width), F32)
    main = gain_scratch[:, pl.ds(pl.multiple_of(member * CHUNK, 128), CHUNK)]
    tail = jnp.concatenate(
        [gain[:, first:first + size] for first, size in tails] + [jnp.zeros((1, spare), F32)], axis=1
    )
    feature = lax.broadcasted_iota(jnp.int32, main.shape, 1)
    own_gain_ref[...] = jnp.where(is_last, tail, jnp.where(feature < MAIN, main, 0.0))


def prepare(experts, slots, member, ids, weights, tokens, gain):
    width, rows = tokens.shape
    return pl.pallas_call(
        functools.partial(prepare_kernel, experts, slots),
        out_shape=[
            shape((experts * slots, rows)),
            shape((3 * rows, experts * slots)),
            shape((rows, CHUNK)),
            shape((1, CHUNK), F32),
        ],
        in_specs=[SMEM] + [VMEM] * 4,
        out_specs=[VMEM] * 4,
        scratch_shapes=[pltpu.VMEM((1, (width // CHUNK + 1) * CHUNK), F32)],
        compiler_params=pltpu.CompilerParams(vmem_limit_bytes=24 * 1024 * 1024),
    )(member.reshape(1), ids, weights, tokens, gain)


def attend(pos_ref, query_ref, kv_refs, carry, diagonal=False):
    rows = kv_refs[0].shape[1] - EXTRA
    mine = pos_ref[0].astype(F32)
    key_side = lax.broadcasted_iota(jnp.int32, (rows, 2 * HEAD_WIDTH), 1) < HEAD_WIDTH
    flag_lane = lax.broadcasted_iota(jnp.int32, (rows, 2 * HEAD_WIDTH), 1) == HEAD_WIDTH
    top, mixed = carry
    for _ in range(1):
        keys = []
        vals = []
        for kv_ref, block in [(ref, i) for ref in kv_refs for i in range(ref.shape[0])]:
            marks = kv_ref[block, rows:rows + EXTRA, :].astype(F32)
            base = marks[0:1, 0:1] * 128.0 + marks[0:1, 1:2]
            hidden = jnp.where(base <= mine, 0.0, -1e30)
            kv = kv_ref[block, :rows, :].astype(F32)
            keys.append(jnp.where(key_side, kv, jnp.where(flag_lane, hidden, 0.0)).astype(BF16))
            vals.append(jnp.where(key_side, 1.0, kv).astype(BF16))
        keys = jnp.concatenate(keys, axis=0)
        vals = jnp.concatenate(vals, axis=0)
        scores = dot(query_ref[...], keys, ((1,), (1,)))
        if diagonal:
            own = scores[:, :rows]
            query_row = lax.broadcasted_iota(jnp.int32, own.shape, 0) % rows
            key_row = lax.broadcasted_iota(jnp.int32, own.shape, 1)
            own = jnp.where(key_row <= query_row, own, -1e30)
            scores = jnp.concatenate([own, scores[:, rows:]], axis=1)
        top_new = jnp.maximum(top, jnp.max(scores, axis=1, keepdims=True))
        probs = jnp.exp(scores - top_new).astype(BF16)
        mixed = mixed * jnp.exp(top - top_new) + dot(probs, vals)
        top = top_new
    return top, mixed


def first_attention_kernel(pos_ref, sink_ref, query_ref, *refs):
    *kv_refs, top_ref, mixed_ref = refs
    columns = query_ref.shape[0]
    heads = sink_ref.shape[0]
    top = jnp.concatenate(
        [jnp.full((columns // heads, 1), sink_ref[head], F32) for head in range(heads)], axis=0
    )
    lane = lax.broadcasted_iota(jnp.int32, (columns, 2 * HEAD_WIDTH), 1)
    start = (top, jnp.where(lane < HEAD_WIDTH, 1.0, 0.0))
    top_ref[...], mixed_ref[...] = attend(pos_ref, query_ref, kv_refs, start, True)


def middle_attention_kernel(pos_ref, query_ref, old_top_ref, old_mixed_ref, *refs):
    *kv_refs, top_ref, mixed_ref = refs
    carry = (old_top_ref[...], old_mixed_ref[...])
    top_ref[...], mixed_ref[...] = attend(pos_ref, query_ref, kv_refs, carry)


def last_attention_kernel(pos_ref, query_ref, old_top_ref, old_mixed_ref, w_ref, *refs):
    *kv_refs, out_ref = refs
    width = w_ref.shape[0]
    columns = query_ref.shape[0]
    rows = out_ref.shape[1]
    _, mixed = attend(pos_ref, query_ref, kv_refs, (old_top_ref[...], old_mixed_ref[...]))
    heads = (mixed[:, HEAD_WIDTH:] / mixed[:, :HEAD_WIDTH]).astype(BF16)
    stacked = jnp.concatenate(
        [heads[head * rows:(head + 1) * rows] for head in range(columns // rows)], axis=1
    )
    full = width // CHUNK
    for place in range(full):
        part = dot(stacked, w_ref[place * CHUNK:(place + 1) * CHUNK, :], ((1,), (1,)))
        out_ref[place] = part.astype(BF16)
    tail = jnp.concatenate(
        [w_ref[first:first + size, :] for first, size in tail_spans(width)], axis=0
    )
    out_ref[full] = jnp.zeros((rows, CHUNK), BF16)
    out_ref[full, :, :tail.shape[0]] = dot(stacked, tail, ((1,), (1,))).astype(BF16)


def dispatch_kernel(
    parts_ref, tokens_ref, gain_ref, gather_ref, attended_ref, residual_ref, out_ref
):
    total = parts_ref[0].astype(F32)
    for index in range(1, parts_ref.shape[0]):
        total = total + parts_ref[index].astype(F32)
    lane = lax.broadcasted_iota(jnp.int32, total.shape, 1)
    attended = jnp.where(lane < MAIN, total, 0.0).astype(BF16)
    attended_ref[...] = attended
    residual = tokens_ref[...].astype(F32) + attended.astype(F32)
    residual_ref[...] = residual
    left = jnp.sum(residual * residual, axis=1, keepdims=True)
    moe_in = residual * gain_ref[...]
    for place in range(3):
        rounded = left.astype(BF16).astype(F32)
        moe_in = jnp.where(lane == MAIN + place, rounded, moe_in)
        left = left - rounded
    out_ref[...] = dot(gather_ref[...], moe_in.astype(BF16)).astype(BF16)


def expert_kernel(
    width, rows_in_ref, gate_ref, up_ref, down_ref, far_gate_ref, far_up_ref, late_ref,
    out_ref, rows_ref, held_ref,
):
    units = gate_ref.shape[0]
    held_ref[:LATE, :] = late_ref[:LATE, :]
    held_ref[LATE:, :] = far_up_ref[...]
    own = (gate_ref, up_ref, down_ref)
    far = (far_gate_ref, held_ref, late_ref.at[pl.ds(LATE, units)])
    full = width // CHUNK
    split = CHUNK - 128
    count = rows_in_ref.shape[1]
    main_lane = lax.broadcasted_iota(jnp.int32, (count, 128), 1) < MAIN - split
    squares = jnp.zeros((count, 128), F32)
    for place in range(full + 1):
        last = rows_in_ref[place, :, split:].astype(F32)
        squares = squares + jnp.where(main_lane, 0.0, last)
        if place < full:
            first = place * CHUNK
            rows_ref[:, first:first + split] = rows_in_ref[place, :, :split]
            rows_ref[:, first + split:first + CHUNK] = jnp.where(main_lane, last, 0.0).astype(BF16)
    squares = jnp.sum(squares, axis=1, keepdims=True)
    scale = lax.rsqrt(squares / width + EPSILON)
    tails = tail_spans(width)
    tail_width = sum(size for _, size in tails)
    tail_rows = rows_in_ref[full, :, :tail_width]

    def columns(refs_in, first, size):
        start = 0
        for ref in refs_in:
            if start <= first < start + ref.shape[1]:
                return ref[:, first - start:first - start + size]
            start += ref.shape[1]

    def tail(refs_in):
        return jnp.concatenate([columns(refs_in, *span) for span in tails], axis=1)

    def product(ref):
        main = dot(rows_ref[...], ref[:, :full * CHUNK], ((1,), (1,)))
        return (main + dot(tail_rows, tail([ref]), ((1,), (1,)))) * scale

    hidden = []
    downs = []
    for gate_ref, up_ref, down_ref in (own, far):
        gate = product(gate_ref)
        up = product(up_ref)
        hidden.append((gate * jax.nn.sigmoid(1.702 * gate) * (up + 1.0)).astype(BF16))
        downs.append([down_ref])
    for place in range(full):
        part = 0.0
        for act, down in zip(hidden, downs):
            part = part + dot(act, columns(down, place * CHUNK, CHUNK))
        out_ref[place] = part.astype(BF16)
    part = 0.0
    for act, down in zip(hidden, downs):
        part = part + dot(act, tail(down))
    out_ref[full] = jnp.zeros(out_ref.shape[1:], BF16)
    out_ref[full, :, :tail_width] = part.astype(BF16)


def run_experts(width, expert_rows, own, far):
    rows = expert_rows.shape[1]
    return pl.pallas_call(
        functools.partial(expert_kernel, width),
        out_shape=shape(expert_rows.shape),
        in_specs=[VMEM] * 7,
        out_specs=VMEM,
        scratch_shapes=[
            pltpu.VMEM((rows, width // CHUNK * CHUNK), BF16),
            pltpu.VMEM(own[1].shape, BF16),
        ],
        compiler_params=pltpu.CompilerParams(vmem_limit_bytes=20 * 1024 * 1024),
    )(expert_rows, *own, *far)


def sum_kernel(groups, parts_ref, out_ref):
    for half, members in enumerate(groups):
        total = parts_ref[members[0]].astype(F32)
        for index in members[1:]:
            total = total + parts_ref[index].astype(F32)
        out_ref[half] = total.astype(BF16)


def combine_kernel(returned_ref, combine_ref, residual_ref, attended_ref, out_ref):
    rows = residual_ref.shape[0]
    mixed = dot(combine_ref[...], returned_ref[...])
    total = mixed[:rows] + mixed[rows:2 * rows] + mixed[2 * rows:]
    out_ref[:, :CHUNK] = attended_ref[...]
    out_ref[:, CHUNK:] = (residual_ref[...] + total).astype(BF16)


def finish_kernel(parts_ref, attended_ref, layer_ref):
    width = attended_ref.shape[1]
    full = width // CHUNK
    for out_ref, at in ((attended_ref, 0), (layer_ref, CHUNK)):
        last = parts_ref[full, :, at:at + CHUNK].astype(F32)
        rest = width - full * CHUNK
        for place in range(full):
            start = rest + place * TAIL
            main = parts_ref[place, :, at:at + MAIN].astype(F32)
            whole = jnp.concatenate([main, last[:, start:start + TAIL]], axis=1)
            out_ref[:, place * CHUNK:(place + 1) * CHUNK] = whole.astype(BF16)
        out_ref[:, full * CHUNK:] = last[:, :rest].astype(BF16)


def exchange(block, axis, groups=None):
    return lax.all_to_all(
        block, axis, split_axis=0, concat_axis=0, tiled=True, axis_index_groups=groups
    )


def local(
    tokens,
    positions,
    norm_attn,
    norm_moe,
    w_query,
    key_matrix,
    value_matrix,
    w_out,
    sinks,
    expert_ids,
    expert_weights,
    w_gate,
    w_up,
    w_down,
):
    ctx_count = lax.axis_size("ctx")
    exp_count = lax.axis_size("exp")
    rows, width = tokens.shape
    heads = sinks.shape[0]
    top = expert_ids.shape[1]
    experts = ctx_count
    slots = rows * top * 3 // (2 * experts)
    member = lax.axis_index("exp")

    swap = [(i, i ^ 2) for i in range(exp_count)]
    gate, up, down = w_gate[0].T, w_up[0].T, w_down[0]

    normed, payload = project_kv(
        positions, tokens.T, norm_attn, key_matrix.T, value_matrix.T
    )
    far_gate = lax.ppermute(gate, "exp", swap)
    late = jnp.concatenate([up[:LATE], down], axis=0)

    def moved(block, x, z, core):
        route = []
        for i in range(ctx_count):
            there = (i // 8 + x) % 4 * 8 + (i // 2 % 4 + z) % 4 * 2 + (i % 2 + core) % 2
            route.append((i, there))
        return lax.ppermute(block, "ctx", route)

    queries = call(query_kernel, shape((heads * rows, 2 * HEAD_WIDTH)), [VMEM, VMEM])(normed, w_query)
    stops = [moved(payload, 0, z, 0) for z in range(1, 4)]
    *stops, queries = lax.optimization_barrier((*stops, queries))
    column = jnp.stack([payload] + stops)
    column_far = moved(column, 0, 0, 1)
    planes = [moved(column, x, 0, 0) for x in range(1, 4)]
    state = [shape((heads * rows, 1), F32), shape((heads * rows, 2 * HEAD_WIDTH), F32)]
    carried = call(first_attention_kernel, state, [SMEM, SMEM] + [VMEM] * 3)(
        positions, sinks, queries, column, column_far
    )
    prepared = prepare(
        experts, slots, member, expert_ids.T, expert_weights.T, tokens.T, norm_moe
    )
    *planes, top_row, mixed, gather_table, combine_table, own_tokens, own_gain, late = (
        lax.optimization_barrier((*planes, *carried, *prepared, late))
    )
    planes_far = [moved(plane, 0, 0, 1) for plane in planes]
    carried = call(middle_attention_kernel, state, [SMEM] + [VMEM] * 6)(
        positions, queries, top_row, mixed, *planes
    )
    top_row, mixed, far_gate = lax.optimization_barrier((*carried, far_gate))
    far_up = lax.ppermute(up[LATE:], "exp", swap)
    partial_sums = call(
        last_attention_kernel, shape((exp_count, rows, CHUNK)), [SMEM] + [VMEM] * 7
    )(positions, queries, top_row, mixed, w_out.T, *planes_far)
    partial_sums, far_up, late = lax.optimization_barrier((partial_sums, far_up, late))
    parts = exchange(partial_sums, "exp")
    attended, residual, outgoing = call(
        dispatch_kernel,
        [shape((rows, CHUNK)), shape((rows, CHUNK), F32), shape((experts * slots, CHUNK))],
        [VMEM] * 4,
    )(parts, own_tokens, own_gain, gather_table)
    arrived = exchange(outgoing.reshape(ctx_count, slots, CHUNK), "ctx")
    far_late = lax.ppermute(late, "exp", swap)
    arrived, far_late = lax.optimization_barrier((arrived, far_late))
    halves = arrived.reshape(1, 2, 1, ctx_count * slots // 2, CHUNK)
    spread = jnp.broadcast_to(halves, (exp_count // 4, 2, 2) + halves.shape[3:])
    expert_rows = exchange(spread.reshape((exp_count,) + halves.shape[3:]), "exp")
    products = run_experts(width, expert_rows, (gate, up, down), (far_gate, far_up, far_late))
    product_parts = exchange(products, "exp")
    groups = [[i for i in range(exp_count) if (i >> 1) & 1 == half] for half in range(2)]
    summed = call(
        functools.partial(sum_kernel, groups),
        shape((2, ctx_count * slots // 2, CHUNK)),
        [VMEM],
    )(product_parts)
    returned = exchange(summed.reshape(ctx_count, slots, CHUNK), "ctx")
    final = call(combine_kernel, shape((rows, 2 * CHUNK)), [VMEM] * 4)(
        returned.reshape(experts * slots, CHUNK), combine_table, residual, attended
    )
    final = exchange(final.reshape(exp_count, rows // exp_count, 2 * CHUNK), "exp")
    out = shape((rows // exp_count, width))
    return tuple(call(finish_kernel, [out, out], [VMEM])(final))


def solution(mesh):
    in_specs = (
        P("ctx", None),
        P("ctx"),
        P(),
        P(),
        P(None, "exp"),
        P(None, "exp"),
        P(None, "exp"),
        P("exp", None),
        P("exp"),
        P("ctx", None),
        P("ctx", None),
        P("ctx", None, "exp"),
        P("ctx", None, "exp"),
        P("ctx", "exp", None),
    )
    out_specs = (P(("ctx", "exp"), None), P(("ctx", "exp"), None))
    return jax.shard_map(local, mesh=mesh, in_specs=in_specs, out_specs=out_specs, check_vma=False)
```

```python
import functools

import jax
import jax.numpy as jnp
from jax import lax
from jax.experimental import pallas as pl
from jax.experimental.pallas import tpu as pltpu
from jax.sharding import PartitionSpec as P

HEAD_WIDTH = 64
EPSILON = 1e-05
CHUNK = 384
TAIL = 16
LATE = 48
MAIN = CHUNK - TAIL
EXTRA = 16
BF16 = jnp.bfloat16
F32 = jnp.float32
VMEM = pl.BlockSpec(memory_space=pltpu.VMEM)
SMEM = pl.BlockSpec(memory_space=pltpu.SMEM)
HBM = pl.BlockSpec(memory_space=pltpu.HBM)


def in_hbm(array):
    return pltpu.with_memory_space_constraint(array, pltpu.HBM)


def call(kernel, out_shapes, in_specs, vmem_mib=24):
    single = not isinstance(out_shapes, (list, tuple))
    out_specs = VMEM if single else [VMEM] * len(out_shapes)
    return pl.pallas_call(
        kernel,
        out_shape=out_shapes,
        in_specs=in_specs,
        out_specs=out_specs,
        compiler_params=pltpu.CompilerParams(vmem_limit_bytes=vmem_mib * 1024 * 1024),
    )


def shape(dims, dtype=BF16):
    return jax.ShapeDtypeStruct(dims, dtype)


def dot(a, b, contract=((1,), (0,))):
    return lax.dot_general(a, b, (contract, ((), ())), preferred_element_type=F32)


def spans(width):
    return [(start, min(CHUNK, width - start)) for start in range(0, width, CHUNK)]


def fetch(sources, held, sems):
    copies = [
        pltpu.make_async_copy(source, target, sems.at[index])
        for index, (source, target) in enumerate(zip(sources, held))
    ]
    for copy in copies:
        copy.start()
    return copies


def tail_spans(width):
    full = width // CHUNK
    return [(full * CHUNK, width - full * CHUNK)] + [
        (place * CHUNK + MAIN, TAIL) for place in range(full)
    ]


def kv_kernel(
    pos_ref, tokens_hbm, gain_hbm, key_hbm, value_hbm, normed_ref, payload_ref,
    tokens_ref, gain_ref, key_ref, value_ref, sems,
):
    sources = (tokens_hbm, gain_hbm, key_hbm, value_hbm)
    copies = fetch(sources, (tokens_ref, gain_ref, key_ref, value_ref), sems)
    rows = tokens_ref.shape[1]
    copies[0].wait()
    values = tokens_ref[...].T.astype(F32)
    mean_square = jnp.mean(values * values, axis=-1, keepdims=True)
    copies[1].wait()
    normed = (values * lax.rsqrt(mean_square + EPSILON) * gain_ref[...][None, :]).astype(BF16)
    normed_ref[...] = normed
    copies[2].wait()
    keys = dot(normed, key_ref[...], ((1,), (1,)))
    copies[3].wait()
    vals = dot(normed, value_ref[...], ((1,), (1,)))
    payload_ref[:rows, :] = jnp.concatenate([keys, vals], axis=1).astype(BF16)
    base = pos_ref[0]
    lane = lax.broadcasted_iota(jnp.int32, (EXTRA, payload_ref.shape[1]), 1)
    marks = jnp.where(lane == 0, base // 128, jnp.where(lane == 1, base % 128, 0))
    payload_ref[rows:, :] = marks.astype(F32).astype(BF16)


def project_kv(positions, tokens, gain, keys, vals):
    width, rows = tokens.shape
    arrays = (tokens, gain, keys, vals)
    return pl.pallas_call(
        kv_kernel,
        out_shape=[shape((rows, width)), shape((rows + EXTRA, 2 * HEAD_WIDTH))],
        in_specs=[SMEM] + [HBM] * 4,
        out_specs=[VMEM, VMEM],
        scratch_shapes=[pltpu.VMEM(a.shape, a.dtype) for a in arrays]
        + [pltpu.SemaphoreType.DMA((4,))],
        compiler_params=pltpu.CompilerParams(vmem_limit_bytes=32 * 1024 * 1024),
    )(in_hbm(positions), *[in_hbm(a) for a in arrays])


def query_kernel(normed_ref, w_ref, out_ref):
    rows = normed_ref.shape[0]
    heads = w_ref.shape[1] // HEAD_WIDTH
    queries = dot(normed_ref[...], w_ref[...]).astype(BF16)
    queries = queries * jnp.asarray(HEAD_WIDTH ** (-0.5), BF16)
    lane = lax.broadcasted_iota(jnp.int32, (rows, HEAD_WIDTH), 1)
    flag = jnp.where(lane == 0, 1.0, 0.0).astype(BF16)
    for head in range(heads):
        own = queries[:, head * HEAD_WIDTH:(head + 1) * HEAD_WIDTH]
        out_ref[head * rows:(head + 1) * rows, :] = jnp.concatenate([own, flag], axis=1)


def upright(ref):
    spare = jnp.zeros((8 - ref.shape[0], ref.shape[1]), F32)
    return jnp.concatenate([ref[...].astype(F32), spare], axis=0).T


def prepare_kernel(
    experts, slots, member_ref, ids_ref, weights_ref, tokens_ref, gain_ref,
    gather_ref, combine_ref, own_tokens_ref, own_gain_ref, gain_scratch,
):
    top, rows = ids_ref.shape
    cells = experts * slots
    ids, weights = upright(ids_ref), upright(weights_ref)
    expert_lane = lax.broadcasted_iota(jnp.int32, (rows, experts), 1).astype(F32)
    chosen = [(ids[:, k:k + 1] == expert_lane).astype(F32) for k in range(top)]
    named = functools.reduce(jnp.add, chosen)
    below = lax.broadcasted_iota(jnp.int32, (rows, rows), 1) < lax.broadcasted_iota(
        jnp.int32, (rows, rows), 0
    )
    place = dot(below.astype(BF16), named.astype(BF16)) + expert_lane * slots
    cell = lax.broadcasted_iota(jnp.int32, (rows, cells), 1).astype(F32)
    filled = jnp.zeros((rows, cells), F32)
    scaled = jnp.zeros((rows, cells), F32)
    for k in range(top):
        target = jnp.sum(chosen[k] * place, axis=1, keepdims=True)
        match = cell == target
        filled = jnp.where(match, 1.0, filled)
        scaled = jnp.where(match, weights[:, k:k + 1], scaled)
    gather_ref[...] = filled.T.astype(BF16)
    for part in range(3):
        rounded = scaled.astype(BF16)
        combine_ref[part * rows:(part + 1) * rows, :] = rounded
        scaled = scaled - rounded.astype(F32)

    width = tokens_ref.shape[0]
    full = width // CHUNK
    rest = width - full * CHUNK
    tails = tail_spans(width)
    spare = CHUNK - sum(size for _, size in tails)
    member = member_ref[0]
    is_last = jnp.full((1, 1), member, jnp.int32) == full
    start = pl.multiple_of(member * CHUNK, rest)
    second = pl.multiple_of(jnp.minimum(start + CHUNK - rest, full * CHUNK), rest)
    main = jnp.concatenate(
        [tokens_ref[pl.ds(start, rest), :], tokens_ref[pl.ds(second, CHUNK - rest), :]], axis=0
    ).astype(F32)
    tail = jnp.concatenate(
        [tokens_ref[first:first + size, :].astype(F32) for first, size in tails]
        + [jnp.zeros((spare, rows), F32)],
        axis=0,
    )
    feature = lax.broadcasted_iota(jnp.int32, main.shape, 0)
    own = jnp.where(is_last, tail, jnp.where(feature < MAIN, main, 0.0))
    own_tokens_ref[...] = own.T.astype(BF16)

    gain = gain_ref[...][None, :]
    gain_scratch[:, :width] = gain
    gain_scratch[:, width:] = jnp.zeros((1, gain_scratch.shape[1] - width), F32)
    main = gain_scratch[:, pl.ds(pl.multiple_of(member * CHUNK, 128), CHUNK)]
    tail = jnp.concatenate(
        [gain[:, first:first + size] for first, size in tails] + [jnp.zeros((1, spare), F32)], axis=1
    )
    feature = lax.broadcasted_iota(jnp.int32, main.shape, 1)
    own_gain_ref[...] = jnp.where(is_last, tail, jnp.where(feature < MAIN, main, 0.0))


def prepare(experts, slots, member, ids, weights, tokens, gain):
    width, rows = tokens.shape
    return pl.pallas_call(
        functools.partial(prepare_kernel, experts, slots),
        out_shape=[
            shape((experts * slots, rows)),
            shape((3 * rows, experts * slots)),
            shape((rows, CHUNK)),
            shape((1, CHUNK), F32),
        ],
        in_specs=[SMEM] + [VMEM] * 4,
        out_specs=[VMEM] * 4,
        scratch_shapes=[pltpu.VMEM((1, (width // CHUNK + 1) * CHUNK), F32)],
        compiler_params=pltpu.CompilerParams(vmem_limit_bytes=24 * 1024 * 1024),
    )(member.reshape(1), ids, weights, tokens, gain)


def attend(pos_ref, query_ref, kv_refs, carry, diagonal=False):
    rows = kv_refs[0].shape[1] - EXTRA
    mine = pos_ref[0].astype(F32)
    key_side = lax.broadcasted_iota(jnp.int32, (rows, 2 * HEAD_WIDTH), 1) < HEAD_WIDTH
    flag_lane = lax.broadcasted_iota(jnp.int32, (rows, 2 * HEAD_WIDTH), 1) == HEAD_WIDTH
    top, mixed = carry
    for _ in range(1):
        keys = []
        vals = []
        for kv_ref, block in [(ref, i) for ref in kv_refs for i in range(ref.shape[0])]:
            marks = kv_ref[block, rows:rows + EXTRA, :].astype(F32)
            base = marks[0:1, 0:1] * 128.0 + marks[0:1, 1:2]
            hidden = jnp.where(base <= mine, 0.0, -1e30)
            kv = kv_ref[block, :rows, :].astype(F32)
            keys.append(jnp.where(key_side, kv, jnp.where(flag_lane, hidden, 0.0)).astype(BF16))
            vals.append(jnp.where(key_side, 1.0, kv).astype(BF16))
        keys = jnp.concatenate(keys, axis=0)
        vals = jnp.concatenate(vals, axis=0)
        scores = dot(query_ref[...], keys, ((1,), (1,)))
        if diagonal:
            own = scores[:, :rows]
            query_row = lax.broadcasted_iota(jnp.int32, own.shape, 0) % rows
            key_row = lax.broadcasted_iota(jnp.int32, own.shape, 1)
            own = jnp.where(key_row <= query_row, own, -1e30)
            scores = jnp.concatenate([own, scores[:, rows:]], axis=1)
        top_new = jnp.maximum(top, jnp.max(scores, axis=1, keepdims=True))
        probs = jnp.exp(scores - top_new).astype(BF16)
        mixed = mixed * jnp.exp(top - top_new) + dot(probs, vals)
        top = top_new
    return top, mixed


def first_attention_kernel(pos_ref, sink_ref, query_ref, *refs):
    *kv_refs, top_ref, mixed_ref = refs
    columns = query_ref.shape[0]
    heads = sink_ref.shape[0]
    top = jnp.concatenate(
        [jnp.full((columns // heads, 1), sink_ref[head], F32) for head in range(heads)], axis=0
    )
    lane = lax.broadcasted_iota(jnp.int32, (columns, 2 * HEAD_WIDTH), 1)
    start = (top, jnp.where(lane < HEAD_WIDTH, 1.0, 0.0))
    top_ref[...], mixed_ref[...] = attend(pos_ref, query_ref, kv_refs, start, True)


def middle_attention_kernel(pos_ref, query_ref, old_top_ref, old_mixed_ref, *refs):
    *kv_refs, top_ref, mixed_ref = refs
    carry = (old_top_ref[...], old_mixed_ref[...])
    top_ref[...], mixed_ref[...] = attend(pos_ref, query_ref, kv_refs, carry)


def last_attention_kernel(pos_ref, query_ref, old_top_ref, old_mixed_ref, w_ref, *refs):
    *kv_refs, out_ref = refs
    width = w_ref.shape[0]
    columns = query_ref.shape[0]
    rows = out_ref.shape[1]
    _, mixed = attend(pos_ref, query_ref, kv_refs, (old_top_ref[...], old_mixed_ref[...]))
    heads = (mixed[:, HEAD_WIDTH:] / mixed[:, :HEAD_WIDTH]).astype(BF16)
    stacked = jnp.concatenate(
        [heads[head * rows:(head + 1) * rows] for head in range(columns // rows)], axis=1
    )
    full = width // CHUNK
    for place in range(full):
        part = dot(stacked, w_ref[place * CHUNK:(place + 1) * CHUNK, :], ((1,), (1,)))
        out_ref[place] = part.astype(BF16)
    tail = jnp.concatenate(
        [w_ref[first:first + size, :] for first, size in tail_spans(width)], axis=0
    )
    out_ref[full] = jnp.zeros((rows, CHUNK), BF16)
    out_ref[full, :, :tail.shape[0]] = dot(stacked, tail, ((1,), (1,))).astype(BF16)


def dispatch_kernel(
    parts_ref, tokens_ref, gain_ref, gather_ref, attended_ref, residual_ref, out_ref
):
    total = parts_ref[0].astype(F32)
    for index in range(1, parts_ref.shape[0]):
        total = total + parts_ref[index].astype(F32)
    lane = lax.broadcasted_iota(jnp.int32, total.shape, 1)
    attended = jnp.where(lane < MAIN, total, 0.0).astype(BF16)
    attended_ref[...] = attended
    residual = tokens_ref[...].astype(F32) + attended.astype(F32)
    residual_ref[...] = residual
    left = jnp.sum(residual * residual, axis=1, keepdims=True)
    moe_in = residual * gain_ref[...]
    for place in range(3):
        rounded = left.astype(BF16).astype(F32)
        moe_in = jnp.where(lane == MAIN + place, rounded, moe_in)
        left = left - rounded
    out_ref[...] = dot(gather_ref[...], moe_in.astype(BF16)).astype(BF16)


def expert_kernel(
    width, rows_in_ref, gate_ref, up_ref, down_ref, far_gate_ref, far_up_ref, late_ref,
    out_ref, rows_ref, held_ref,
):
    units = gate_ref.shape[0]
    held_ref[:LATE, :] = late_ref[:LATE, :]
    held_ref[LATE:, :] = far_up_ref[...]
    own = (gate_ref, up_ref, down_ref)
    far = (far_gate_ref, held_ref, late_ref.at[pl.ds(LATE, units)])
    full = width // CHUNK
    split = CHUNK - 128
    count = rows_in_ref.shape[1]
    main_lane = lax.broadcasted_iota(jnp.int32, (count, 128), 1) < MAIN - split
    squares = jnp.zeros((count, 128), F32)
    for place in range(full + 1):
        last = rows_in_ref[place, :, split:].astype(F32)
        squares = squares + jnp.where(main_lane, 0.0, last)
        if place < full:
            first = place * CHUNK
            rows_ref[:, first:first + split] = rows_in_ref[place, :, :split]
            rows_ref[:, first + split:first + CHUNK] = jnp.where(main_lane, last, 0.0).astype(BF16)
    squares = jnp.sum(squares, axis=1, keepdims=True)
    scale = lax.rsqrt(squares / width + EPSILON)
    tails = tail_spans(width)
    tail_width = sum(size for _, size in tails)
    tail_rows = rows_in_ref[full, :, :tail_width]

    def columns(refs_in, first, size):
        start = 0
        for ref in refs_in:
            if start <= first < start + ref.shape[1]:
                return ref[:, first - start:first - start + size]
            start += ref.shape[1]

    def tail(refs_in):
        return jnp.concatenate([columns(refs_in, *span) for span in tails], axis=1)

    def product(ref):
        main = dot(rows_ref[...], ref[:, :full * CHUNK], ((1,), (1,)))
        return (main + dot(tail_rows, tail([ref]), ((1,), (1,)))) * scale

    hidden = []
    downs = []
    for gate_ref, up_ref, down_ref in (own, far):
        gate = product(gate_ref)
        up = product(up_ref)
        hidden.append((gate * jax.nn.sigmoid(1.702 * gate) * (up + 1.0)).astype(BF16))
        downs.append([down_ref])
    for place in range(full):
        part = 0.0
        for act, down in zip(hidden, downs):
            part = part + dot(act, columns(down, place * CHUNK, CHUNK))
        out_ref[place] = part.astype(BF16)
    part = 0.0
    for act, down in zip(hidden, downs):
        part = part + dot(act, tail(down))
    out_ref[full] = jnp.zeros(out_ref.shape[1:], BF16)
    out_ref[full, :, :tail_width] = part.astype(BF16)


def run_experts(width, expert_rows, own, far):
    rows = expert_rows.shape[1]
    return pl.pallas_call(
        functools.partial(expert_kernel, width),
        out_shape=shape(expert_rows.shape),
        in_specs=[VMEM] * 7,
        out_specs=VMEM,
        scratch_shapes=[
            pltpu.VMEM((rows, width // CHUNK * CHUNK), BF16),
            pltpu.VMEM(own[1].shape, BF16),
        ],
        compiler_params=pltpu.CompilerParams(vmem_limit_bytes=20 * 1024 * 1024),
    )(expert_rows, *own, *far)


def sum_kernel(groups, parts_ref, out_ref):
    for half, members in enumerate(groups):
        total = parts_ref[members[0]].astype(F32)
        for index in members[1:]:
            total = total + parts_ref[index].astype(F32)
        out_ref[half] = total.astype(BF16)


def combine_kernel(returned_ref, combine_ref, residual_ref, attended_ref, out_ref):
    rows = residual_ref.shape[0]
    mixed = dot(combine_ref[...], returned_ref[...])
    total = mixed[:rows] + mixed[rows:2 * rows] + mixed[2 * rows:]
    out_ref[:, :CHUNK] = attended_ref[...]
    out_ref[:, CHUNK:] = (residual_ref[...] + total).astype(BF16)


def finish_kernel(parts_ref, attended_ref, layer_ref):
    width = attended_ref.shape[1]
    full = width // CHUNK
    for out_ref, at in ((attended_ref, 0), (layer_ref, CHUNK)):
        last = parts_ref[full, :, at:at + CHUNK].astype(F32)
        rest = width - full * CHUNK
        for place in range(full):
            start = rest + place * TAIL
            main = parts_ref[place, :, at:at + MAIN].astype(F32)
            whole = jnp.concatenate([main, last[:, start:start + TAIL]], axis=1)
            out_ref[:, place * CHUNK:(place + 1) * CHUNK] = whole.astype(BF16)
        out_ref[:, full * CHUNK:] = last[:, :rest].astype(BF16)


def exchange(block, axis, groups=None):
    return lax.all_to_all(
        block, axis, split_axis=0, concat_axis=0, tiled=True, axis_index_groups=groups
    )


def local(
    tokens,
    positions,
    norm_attn,
    norm_moe,
    w_query,
    key_matrix,
    value_matrix,
    w_out,
    sinks,
    expert_ids,
    expert_weights,
    w_gate,
    w_up,
    w_down,
):
    ctx_count = lax.axis_size("ctx")
    exp_count = lax.axis_size("exp")
    rows, width = tokens.shape
    heads = sinks.shape[0]
    top = expert_ids.shape[1]
    experts = ctx_count
    slots = rows * top * 3 // (2 * experts)
    member = lax.axis_index("exp")

    swap = [(i, i ^ 2) for i in range(exp_count)]
    gate, up, down = w_gate[0].T, w_up[0].T, w_down[0]

    normed, payload = project_kv(
        positions, tokens.T, norm_attn, key_matrix.T, value_matrix.T
    )
    far_gate = lax.ppermute(gate, "exp", swap)
    late = jnp.concatenate([up[:LATE], down], axis=0)

    def moved(block, x, z, core):
        route = []
        for i in range(ctx_count):
            there = (i // 8 + x) % 4 * 8 + (i // 2 % 4 + z) % 4 * 2 + (i % 2 + core) % 2
            route.append((i, there))
        return lax.ppermute(block, "ctx", route)

    queries = call(query_kernel, shape((heads * rows, 2 * HEAD_WIDTH)), [VMEM, VMEM])(normed, w_query)
    stops = [moved(payload, 0, z, 0) for z in range(1, 4)]
    *stops, queries = lax.optimization_barrier((*stops, queries))
    column = jnp.stack([payload] + stops)
    column_far = moved(column, 0, 0, 1)
    planes = [moved(column, x, 0, 0) for x in range(1, 4)]
    state = [shape((heads * rows, 1), F32), shape((heads * rows, 2 * HEAD_WIDTH), F32)]
    carried = call(first_attention_kernel, state, [SMEM, SMEM] + [VMEM] * 3)(
        positions, sinks, queries, column, column_far
    )
    prepared = prepare(
        experts, slots, member, expert_ids.T, expert_weights.T, tokens.T, norm_moe
    )
    *planes, top_row, mixed, gather_table, combine_table, own_tokens, own_gain, late = (
        lax.optimization_barrier((*planes, *carried, *prepared, late))
    )
    planes_far = [moved(plane, 0, 0, 1) for plane in planes]
    carried = call(middle_attention_kernel, state, [SMEM] + [VMEM] * 6)(
        positions, queries, top_row, mixed, *planes
    )
    top_row, mixed, far_gate = lax.optimization_barrier((*carried, far_gate))
    far_up = lax.ppermute(up[LATE:], "exp", swap)
    partial_sums = call(
        last_attention_kernel, shape((exp_count, rows, CHUNK)), [SMEM] + [VMEM] * 7
    )(positions, queries, top_row, mixed, w_out.T, *planes_far)
    partial_sums, far_up, late = lax.optimization_barrier((partial_sums, far_up, late))
    parts = exchange(partial_sums, "exp")
    attended, residual, outgoing = call(
        dispatch_kernel,
        [shape((rows, CHUNK)), shape((rows, CHUNK), F32), shape((experts * slots, CHUNK))],
        [VMEM] * 4,
    )(parts, own_tokens, own_gain, gather_table)
    arrived = exchange(outgoing.reshape(ctx_count, slots, CHUNK), "ctx")
    far_late = lax.ppermute(late, "exp", swap)
    arrived, far_late = lax.optimization_barrier((arrived, far_late))
    halves = arrived.reshape(1, 2, 1, ctx_count * slots // 2, CHUNK)
    spread = jnp.broadcast_to(halves, (exp_count // 4, 2, 2) + halves.shape[3:])
    expert_rows = exchange(spread.reshape((exp_count,) + halves.shape[3:]), "exp")
    products = run_experts(width, expert_rows, (gate, up, down), (far_gate, far_up, far_late))
    product_parts = exchange(products, "exp")
    groups = [[i for i in range(exp_count) if (i >> 1) & 1 == half] for half in range(2)]
    summed = call(
        functools.partial(sum_kernel, groups),
        shape((2, ctx_count * slots // 2, CHUNK)),
        [VMEM],
    )(product_parts)
    returned = exchange(summed.reshape(ctx_count, slots, CHUNK), "ctx")
    final = call(combine_kernel, shape((rows, 2 * CHUNK)), [VMEM] * 4)(
        returned.reshape(experts * slots, CHUNK), combine_table, residual, attended
    )
    final = exchange(final.reshape(exp_count, rows // exp_count, 2 * CHUNK), "exp")
    out = shape((rows // exp_count, width))
    return tuple(call(finish_kernel, [out, out], [VMEM])(final))


def solution(mesh):
    in_specs = (
        P("ctx", None),
        P("ctx"),
        P(),
        P(),
        P(None, "exp"),
        P(None, "exp"),
        P(None, "exp"),
        P("exp", None),
        P("exp"),
        P("ctx", None),
        P("ctx", None),
        P("ctx", None, "exp"),
        P("ctx", None, "exp"),
        P("ctx", "exp", None),
    )
    out_specs = (P(("ctx", "exp"), None), P(("ctx", "exp"), None))
    return jax.shard_map(local, mesh=mesh, in_specs=in_specs, out_specs=out_specs, check_vma=False)
```

```python
import functools

import jax
import jax.numpy as jnp
from jax import lax
from jax.experimental import pallas as pl
from jax.experimental.pallas import tpu as pltpu
from jax.sharding import PartitionSpec as P

HEAD_WIDTH = 64
EPSILON = 1e-05
CHUNK = 384
TAIL = 16
LATE = 48
MAIN = CHUNK - TAIL
EXTRA = 16
BF16 = jnp.bfloat16
F32 = jnp.float32
VMEM = pl.BlockSpec(memory_space=pltpu.VMEM)
SMEM = pl.BlockSpec(memory_space=pltpu.SMEM)
HBM = pl.BlockSpec(memory_space=pltpu.HBM)


def in_hbm(array):
    return pltpu.with_memory_space_constraint(array, pltpu.HBM)


def call(kernel, out_shapes, in_specs, vmem_mib=24):
    single = not isinstance(out_shapes, (list, tuple))
    out_specs = VMEM if single else [VMEM] * len(out_shapes)
    return pl.pallas_call(
        kernel,
        out_shape=out_shapes,
        in_specs=in_specs,
        out_specs=out_specs,
        compiler_params=pltpu.CompilerParams(vmem_limit_bytes=vmem_mib * 1024 * 1024),
    )


def shape(dims, dtype=BF16):
    return jax.ShapeDtypeStruct(dims, dtype)


def dot(a, b, contract=((1,), (0,))):
    return lax.dot_general(a, b, (contract, ((), ())), preferred_element_type=F32)


def spans(width):
    return [(start, min(CHUNK, width - start)) for start in range(0, width, CHUNK)]


def fetch(sources, held, sems):
    copies = [
        pltpu.make_async_copy(source, target, sems.at[index])
        for index, (source, target) in enumerate(zip(sources, held))
    ]
    for copy in copies:
        copy.start()
    return copies


def tail_spans(width):
    full = width // CHUNK
    return [(full * CHUNK, width - full * CHUNK)] + [
        (place * CHUNK + MAIN, TAIL) for place in range(full)
    ]


def kv_kernel(
    pos_ref, tokens_hbm, gain_hbm, key_hbm, value_hbm, normed_ref, payload_ref,
    tokens_ref, gain_ref, key_ref, value_ref, sems,
):
    sources = (tokens_hbm, gain_hbm, key_hbm, value_hbm)
    copies = fetch(sources, (tokens_ref, gain_ref, key_ref, value_ref), sems)
    rows = tokens_ref.shape[1]
    copies[0].wait()
    values = tokens_ref[...].T.astype(F32)
    mean_square = jnp.mean(values * values, axis=-1, keepdims=True)
    copies[1].wait()
    normed = (values * lax.rsqrt(mean_square + EPSILON) * gain_ref[...][None, :]).astype(BF16)
    normed_ref[...] = normed
    copies[2].wait()
    keys = dot(normed, key_ref[...], ((1,), (1,)))
    copies[3].wait()
    vals = dot(normed, value_ref[...], ((1,), (1,)))
    payload_ref[:rows, :] = jnp.concatenate([keys, vals], axis=1).astype(BF16)
    base = pos_ref[0]
    lane = lax.broadcasted_iota(jnp.int32, (EXTRA, payload_ref.shape[1]), 1)
    marks = jnp.where(lane == 0, base // 128, jnp.where(lane == 1, base % 128, 0))
    payload_ref[rows:, :] = marks.astype(F32).astype(BF16)


def project_kv(positions, tokens, gain, keys, vals):
    width, rows = tokens.shape
    arrays = (tokens, gain, keys, vals)
    return pl.pallas_call(
        kv_kernel,
        out_shape=[shape((rows, width)), shape((rows + EXTRA, 2 * HEAD_WIDTH))],
        in_specs=[SMEM] + [HBM] * 4,
        out_specs=[VMEM, VMEM],
        scratch_shapes=[pltpu.VMEM(a.shape, a.dtype) for a in arrays]
        + [pltpu.SemaphoreType.DMA((4,))],
        compiler_params=pltpu.CompilerParams(vmem_limit_bytes=32 * 1024 * 1024),
    )(in_hbm(positions), *[in_hbm(a) for a in arrays])


def query_kernel(normed_ref, w_ref, out_ref):
    rows = normed_ref.shape[0]
    heads = w_ref.shape[1] // HEAD_WIDTH
    queries = dot(normed_ref[...], w_ref[...]).astype(BF16)
    queries = queries * jnp.asarray(HEAD_WIDTH ** (-0.5), BF16)
    lane = lax.broadcasted_iota(jnp.int32, (rows, HEAD_WIDTH), 1)
    flag = jnp.where(lane == 0, 1.0, 0.0).astype(BF16)
    for head in range(heads):
        own = queries[:, head * HEAD_WIDTH:(head + 1) * HEAD_WIDTH]
        out_ref[head * rows:(head + 1) * rows, :] = jnp.concatenate([own, flag], axis=1)


def upright(ref):
    spare = jnp.zeros((8 - ref.shape[0], ref.shape[1]), F32)
    return jnp.concatenate([ref[...].astype(F32), spare], axis=0).T


def prepare_kernel(
    experts, slots, member_ref, ids_ref, weights_ref, tokens_ref, gain_ref,
    gather_ref, combine_ref, own_tokens_ref, own_gain_ref, gain_scratch,
):
    top, rows = ids_ref.shape
    cells = experts * slots
    ids, weights = upright(ids_ref), upright(weights_ref)
    expert_lane = lax.broadcasted_iota(jnp.int32, (rows, experts), 1).astype(F32)
    chosen = [(ids[:, k:k + 1] == expert_lane).astype(F32) for k in range(top)]
    named = functools.reduce(jnp.add, chosen)
    below = lax.broadcasted_iota(jnp.int32, (rows, rows), 1) < lax.broadcasted_iota(
        jnp.int32, (rows, rows), 0
    )
    place = dot(below.astype(BF16), named.astype(BF16)) + expert_lane * slots
    cell = lax.broadcasted_iota(jnp.int32, (rows, cells), 1).astype(F32)
    filled = jnp.zeros((rows, cells), F32)
    scaled = jnp.zeros((rows, cells), F32)
    for k in range(top):
        target = jnp.sum(chosen[k] * place, axis=1, keepdims=True)
        match = cell == target
        filled = jnp.where(match, 1.0, filled)
        scaled = jnp.where(match, weights[:, k:k + 1], scaled)
    gather_ref[...] = filled.T.astype(BF16)
    for part in range(3):
        rounded = scaled.astype(BF16)
        combine_ref[part * rows:(part + 1) * rows, :] = rounded
        scaled = scaled - rounded.astype(F32)

    width = tokens_ref.shape[0]
    full = width // CHUNK
    rest = width - full * CHUNK
    tails = tail_spans(width)
    spare = CHUNK - sum(size for _, size in tails)
    member = member_ref[0]
    is_last = jnp.full((1, 1), member, jnp.int32) == full
    start = pl.multiple_of(member * CHUNK, rest)
    second = pl.multiple_of(jnp.minimum(start + CHUNK - rest, full * CHUNK), rest)
    main = jnp.concatenate(
        [tokens_ref[pl.ds(start, rest), :], tokens_ref[pl.ds(second, CHUNK - rest), :]], axis=0
    ).astype(F32)
    tail = jnp.concatenate(
        [tokens_ref[first:first + size, :].astype(F32) for first, size in tails]
        + [jnp.zeros((spare, rows), F32)],
        axis=0,
    )
    feature = lax.broadcasted_iota(jnp.int32, main.shape, 0)
    own = jnp.where(is_last, tail, jnp.where(feature < MAIN, main, 0.0))
    own_tokens_ref[...] = own.T.astype(BF16)

    gain = gain_ref[...][None, :]
    gain_scratch[:, :width] = gain
    gain_scratch[:, width:] = jnp.zeros((1, gain_scratch.shape[1] - width), F32)
    main = gain_scratch[:, pl.ds(pl.multiple_of(member * CHUNK, 128), CHUNK)]
    tail = jnp.concatenate(
        [gain[:, first:first + size] for first, size in tails] + [jnp.zeros((1, spare), F32)], axis=1
    )
    feature = lax.broadcasted_iota(jnp.int32, main.shape, 1)
    own_gain_ref[...] = jnp.where(is_last, tail, jnp.where(feature < MAIN, main, 0.0))


def prepare(experts, slots, member, ids, weights, tokens, gain):
    width, rows = tokens.shape
    return pl.pallas_call(
        functools.partial(prepare_kernel, experts, slots),
        out_shape=[
            shape((experts * slots, rows)),
            shape((3 * rows, experts * slots)),
            shape((rows, CHUNK)),
            shape((1, CHUNK), F32),
        ],
        in_specs=[SMEM] + [VMEM] * 4,
        out_specs=[VMEM] * 4,
        scratch_shapes=[pltpu.VMEM((1, (width // CHUNK + 1) * CHUNK), F32)],
        compiler_params=pltpu.CompilerParams(vmem_limit_bytes=24 * 1024 * 1024),
    )(member.reshape(1), ids, weights, tokens, gain)


def attend(pos_ref, query_ref, kv_refs, carry, diagonal=False):
    rows = kv_refs[0].shape[1] - EXTRA
    mine = pos_ref[0].astype(F32)
    key_side = lax.broadcasted_iota(jnp.int32, (rows, 2 * HEAD_WIDTH), 1) < HEAD_WIDTH
    flag_lane = lax.broadcasted_iota(jnp.int32, (rows, 2 * HEAD_WIDTH), 1) == HEAD_WIDTH
    top, mixed = carry
    for _ in range(1):
        keys = []
        vals = []
        for kv_ref, block in [(ref, i) for ref in kv_refs for i in range(ref.shape[0])]:
            marks = kv_ref[block, rows:rows + EXTRA, :].astype(F32)
            base = marks[0:1, 0:1] * 128.0 + marks[0:1, 1:2]
            hidden = jnp.where(base <= mine, 0.0, -1e30)
            kv = kv_ref[block, :rows, :].astype(F32)
            keys.append(jnp.where(key_side, kv, jnp.where(flag_lane, hidden, 0.0)).astype(BF16))
            vals.append(jnp.where(key_side, 1.0, kv).astype(BF16))
        keys = jnp.concatenate(keys, axis=0)
        vals = jnp.concatenate(vals, axis=0)
        scores = dot(query_ref[...], keys, ((1,), (1,)))
        if diagonal:
            own = scores[:, :rows]
            query_row = lax.broadcasted_iota(jnp.int32, own.shape, 0) % rows
            key_row = lax.broadcasted_iota(jnp.int32, own.shape, 1)
            own = jnp.where(key_row <= query_row, own, -1e30)
            scores = jnp.concatenate([own, scores[:, rows:]], axis=1)
        top_new = jnp.maximum(top, jnp.max(scores, axis=1, keepdims=True))
        probs = jnp.exp(scores - top_new).astype(BF16)
        mixed = mixed * jnp.exp(top - top_new) + dot(probs, vals)
        top = top_new
    return top, mixed


def first_attention_kernel(pos_ref, sink_ref, query_ref, *refs):
    *kv_refs, top_ref, mixed_ref = refs
    columns = query_ref.shape[0]
    heads = sink_ref.shape[0]
    top = jnp.concatenate(
        [jnp.full((columns // heads, 1), sink_ref[head], F32) for head in range(heads)], axis=0
    )
    lane = lax.broadcasted_iota(jnp.int32, (columns, 2 * HEAD_WIDTH), 1)
    start = (top, jnp.where(lane < HEAD_WIDTH, 1.0, 0.0))
    top_ref[...], mixed_ref[...] = attend(pos_ref, query_ref, kv_refs, start, True)


def middle_attention_kernel(pos_ref, query_ref, old_top_ref, old_mixed_ref, *refs):
    *kv_refs, top_ref, mixed_ref = refs
    carry = (old_top_ref[...], old_mixed_ref[...])
    top_ref[...], mixed_ref[...] = attend(pos_ref, query_ref, kv_refs, carry)


def last_attention_kernel(pos_ref, query_ref, old_top_ref, old_mixed_ref, w_ref, *refs):
    *kv_refs, out_ref = refs
    width = w_ref.shape[0]
    columns = query_ref.shape[0]
    rows = out_ref.shape[1]
    _, mixed = attend(pos_ref, query_ref, kv_refs, (old_top_ref[...], old_mixed_ref[...]))
    heads = (mixed[:, HEAD_WIDTH:] / mixed[:, :HEAD_WIDTH]).astype(BF16)
    stacked = jnp.concatenate(
        [heads[head * rows:(head + 1) * rows] for head in range(columns // rows)], axis=1
    )
    full = width // CHUNK
    for place in range(full):
        part = dot(stacked, w_ref[place * CHUNK:(place + 1) * CHUNK, :], ((1,), (1,)))
        out_ref[place] = part.astype(BF16)
    tail = jnp.concatenate(
        [w_ref[first:first + size, :] for first, size in tail_spans(width)], axis=0
    )
    out_ref[full] = jnp.zeros((rows, CHUNK), BF16)
    out_ref[full, :, :tail.shape[0]] = dot(stacked, tail, ((1,), (1,))).astype(BF16)


def dispatch_kernel(
    parts_ref, tokens_ref, gain_ref, gather_ref, attended_ref, residual_ref, out_ref
):
    total = parts_ref[0].astype(F32)
    for index in range(1, parts_ref.shape[0]):
        total = total + parts_ref[index].astype(F32)
    lane = lax.broadcasted_iota(jnp.int32, total.shape, 1)
    attended = jnp.where(lane < MAIN, total, 0.0).astype(BF16)
    attended_ref[...] = attended
    residual = tokens_ref[...].astype(F32) + attended.astype(F32)
    residual_ref[...] = residual
    left = jnp.sum(residual * residual, axis=1, keepdims=True)
    moe_in = residual * gain_ref[...]
    for place in range(3):
        rounded = left.astype(BF16).astype(F32)
        moe_in = jnp.where(lane == MAIN + place, rounded, moe_in)
        left = left - rounded
    out_ref[...] = dot(gather_ref[...], moe_in.astype(BF16)).astype(BF16)


def expert_kernel(
    width, rows_in_ref, gate_ref, up_ref, down_ref, far_gate_ref, far_up_ref, late_ref,
    out_ref, rows_ref, held_ref,
):
    units = gate_ref.shape[0]
    held_ref[:LATE, :] = late_ref[:LATE, :]
    held_ref[LATE:, :] = far_up_ref[...]
    own = (gate_ref, up_ref, down_ref)
    far = (far_gate_ref, held_ref, late_ref.at[pl.ds(LATE, units)])
    full = width // CHUNK
    split = CHUNK - 128
    count = rows_in_ref.shape[1]
    main_lane = lax.broadcasted_iota(jnp.int32, (count, 128), 1) < MAIN - split
    squares = jnp.zeros((count, 128), F32)
    for place in range(full + 1):
        last = rows_in_ref[place, :, split:].astype(F32)
        squares = squares + jnp.where(main_lane, 0.0, last)
        if place < full:
            first = place * CHUNK
            rows_ref[:, first:first + split] = rows_in_ref[place, :, :split]
            rows_ref[:, first + split:first + CHUNK] = jnp.where(main_lane, last, 0.0).astype(BF16)
    squares = jnp.sum(squares, axis=1, keepdims=True)
    scale = lax.rsqrt(squares / width + EPSILON)
    tails = tail_spans(width)
    tail_width = sum(size for _, size in tails)
    tail_rows = rows_in_ref[full, :, :tail_width]

    def columns(refs_in, first, size):
        start = 0
        for ref in refs_in:
            if start <= first < start + ref.shape[1]:
                return ref[:, first - start:first - start + size]
            start += ref.shape[1]

    def tail(refs_in):
        return jnp.concatenate([columns(refs_in, *span) for span in tails], axis=1)

    def product(ref):
        main = dot(rows_ref[...], ref[:, :full * CHUNK], ((1,), (1,)))
        return (main + dot(tail_rows, tail([ref]), ((1,), (1,)))) * scale

    hidden = []
    downs = []
    for gate_ref, up_ref, down_ref in (own, far):
        gate = product(gate_ref)
        up = product(up_ref)
        hidden.append((gate * jax.nn.sigmoid(1.702 * gate) * (up + 1.0)).astype(BF16))
        downs.append([down_ref])
    for place in range(full):
        part = 0.0
        for act, down in zip(hidden, downs):
            part = part + dot(act, columns(down, place * CHUNK, CHUNK))
        out_ref[place] = part.astype(BF16)
    part = 0.0
    for act, down in zip(hidden, downs):
        part = part + dot(act, tail(down))
    out_ref[full] = jnp.zeros(out_ref.shape[1:], BF16)
    out_ref[full, :, :tail_width] = part.astype(BF16)


def run_experts(width, expert_rows, own, far):
    rows = expert_rows.shape[1]
    return pl.pallas_call(
        functools.partial(expert_kernel, width),
        out_shape=shape(expert_rows.shape),
        in_specs=[VMEM] * 7,
        out_specs=VMEM,
        scratch_shapes=[
            pltpu.VMEM((rows, width // CHUNK * CHUNK), BF16),
            pltpu.VMEM(own[1].shape, BF16),
        ],
        compiler_params=pltpu.CompilerParams(vmem_limit_bytes=20 * 1024 * 1024),
    )(expert_rows, *own, *far)


def sum_kernel(groups, parts_ref, out_ref):
    for half, members in enumerate(groups):
        total = parts_ref[members[0]].astype(F32)
        for index in members[1:]:
            total = total + parts_ref[index].astype(F32)
        out_ref[half] = total.astype(BF16)


def combine_kernel(returned_ref, combine_ref, residual_ref, attended_ref, out_ref):
    rows = residual_ref.shape[0]
    mixed = dot(combine_ref[...], returned_ref[...])
    total = mixed[:rows] + mixed[rows:2 * rows] + mixed[2 * rows:]
    out_ref[:, :CHUNK] = attended_ref[...]
    out_ref[:, CHUNK:] = (residual_ref[...] + total).astype(BF16)


def finish_kernel(parts_ref, attended_ref, layer_ref):
    width = attended_ref.shape[1]
    full = width // CHUNK
    for out_ref, at in ((attended_ref, 0), (layer_ref, CHUNK)):
        last = parts_ref[full, :, at:at + CHUNK].astype(F32)
        rest = width - full * CHUNK
        for place in range(full):
            start = rest + place * TAIL
            main = parts_ref[place, :, at:at + MAIN].astype(F32)
            whole = jnp.concatenate([main, last[:, start:start + TAIL]], axis=1)
            out_ref[:, place * CHUNK:(place + 1) * CHUNK] = whole.astype(BF16)
        out_ref[:, full * CHUNK:] = last[:, :rest].astype(BF16)


def exchange(block, axis, groups=None):
    return lax.all_to_all(
        block, axis, split_axis=0, concat_axis=0, tiled=True, axis_index_groups=groups
    )


def local(
    tokens,
    positions,
    norm_attn,
    norm_moe,
    w_query,
    key_matrix,
    value_matrix,
    w_out,
    sinks,
    expert_ids,
    expert_weights,
    w_gate,
    w_up,
    w_down,
):
    ctx_count = lax.axis_size("ctx")
    exp_count = lax.axis_size("exp")
    rows, width = tokens.shape
    heads = sinks.shape[0]
    top = expert_ids.shape[1]
    experts = ctx_count
    slots = rows * top * 3 // (2 * experts)
    member = lax.axis_index("exp")

    swap = [(i, i ^ 2) for i in range(exp_count)]
    gate, up, down = w_gate[0].T, w_up[0].T, w_down[0]

    normed, payload = project_kv(
        positions, tokens.T, norm_attn, key_matrix.T, value_matrix.T
    )
    far_gate = lax.ppermute(gate, "exp", swap)
    late = jnp.concatenate([up[:LATE], down], axis=0)

    def moved(block, x, z, core):
        route = []
        for i in range(ctx_count):
            there = (i // 8 + x) % 4 * 8 + (i // 2 % 4 + z) % 4 * 2 + (i % 2 + core) % 2
            route.append((i, there))
        return lax.ppermute(block, "ctx", route)

    queries = call(query_kernel, shape((heads * rows, 2 * HEAD_WIDTH)), [VMEM, VMEM])(normed, w_query)
    stops = [moved(payload, 0, z, 0) for z in range(1, 4)]
    *stops, queries = lax.optimization_barrier((*stops, queries))
    column = jnp.stack([payload] + stops)
    column_far = moved(column, 0, 0, 1)
    planes = [moved(column, x, 0, 0) for x in range(1, 4)]
    state = [shape((heads * rows, 1), F32), shape((heads * rows, 2 * HEAD_WIDTH), F32)]
    carried = call(first_attention_kernel, state, [SMEM, SMEM] + [VMEM] * 3)(
        positions, sinks, queries, column, column_far
    )
    prepared = prepare(
        experts, slots, member, expert_ids.T, expert_weights.T, tokens.T, norm_moe
    )
    gather_table, combine_table, own_tokens, own_gain = prepared
    *planes, top_row, mixed, late = lax.optimization_barrier((*planes, *carried, late))
    planes_far = [moved(plane, 0, 0, 1) for plane in planes]
    carried = call(middle_attention_kernel, state, [SMEM] + [VMEM] * 6)(
        positions, queries, top_row, mixed, *planes
    )
    top_row, mixed, far_gate = lax.optimization_barrier((*carried, far_gate))
    far_up = lax.ppermute(up[LATE:], "exp", swap)
    partial_sums = call(
        last_attention_kernel, shape((exp_count, rows, CHUNK)), [SMEM] + [VMEM] * 7
    )(positions, queries, top_row, mixed, w_out.T, *planes_far)
    partial_sums, far_up, late = lax.optimization_barrier((partial_sums, far_up, late))
    parts = exchange(partial_sums, "exp")
    attended, residual, outgoing = call(
        dispatch_kernel,
        [shape((rows, CHUNK)), shape((rows, CHUNK), F32), shape((experts * slots, CHUNK))],
        [VMEM] * 4,
    )(parts, own_tokens, own_gain, gather_table)
    arrived = exchange(outgoing.reshape(ctx_count, slots, CHUNK), "ctx")
    far_late = lax.ppermute(late, "exp", swap)
    arrived, far_late = lax.optimization_barrier((arrived, far_late))
    halves = arrived.reshape(1, 2, 1, ctx_count * slots // 2, CHUNK)
    spread = jnp.broadcast_to(halves, (exp_count // 4, 2, 2) + halves.shape[3:])
    expert_rows = exchange(spread.reshape((exp_count,) + halves.shape[3:]), "exp")
    products = run_experts(width, expert_rows, (gate, up, down), (far_gate, far_up, far_late))
    product_parts = exchange(products, "exp")
    groups = [[i for i in range(exp_count) if (i >> 1) & 1 == half] for half in range(2)]
    summed = call(
        functools.partial(sum_kernel, groups),
        shape((2, ctx_count * slots // 2, CHUNK)),
        [VMEM],
    )(product_parts)
    returned = exchange(summed.reshape(ctx_count, slots, CHUNK), "ctx")
    final = call(combine_kernel, shape((rows, 2 * CHUNK)), [VMEM] * 4)(
        returned.reshape(experts * slots, CHUNK), combine_table, residual, attended
    )
    final = exchange(final.reshape(exp_count, rows // exp_count, 2 * CHUNK), "exp")
    out = shape((rows // exp_count, width))
    return tuple(call(finish_kernel, [out, out], [VMEM])(final))


def solution(mesh):
    in_specs = (
        P("ctx", None),
        P("ctx"),
        P(),
        P(),
        P(None, "exp"),
        P(None, "exp"),
        P(None, "exp"),
        P("exp", None),
        P("exp"),
        P("ctx", None),
        P("ctx", None),
        P("ctx", None, "exp"),
        P("ctx", None, "exp"),
        P("ctx", "exp", None),
    )
    out_specs = (P(("ctx", "exp"), None), P(("ctx", "exp"), None))
    return jax.shard_map(local, mesh=mesh, in_specs=in_specs, out_specs=out_specs, check_vma=False)
```

```python
import functools

import jax
import jax.numpy as jnp
from jax import lax
from jax.experimental import pallas as pl
from jax.experimental.pallas import tpu as pltpu
from jax.sharding import PartitionSpec as P

HEAD_WIDTH = 64
EPSILON = 1e-05
CHUNK = 384
TAIL = 16
LATE = 48
MAIN = CHUNK - TAIL
EXTRA = 16
BF16 = jnp.bfloat16
F32 = jnp.float32
VMEM = pl.BlockSpec(memory_space=pltpu.VMEM)
SMEM = pl.BlockSpec(memory_space=pltpu.SMEM)
HBM = pl.BlockSpec(memory_space=pltpu.HBM)


def in_hbm(array):
    return pltpu.with_memory_space_constraint(array, pltpu.HBM)


def call(kernel, out_shapes, in_specs, vmem_mib=24):
    single = not isinstance(out_shapes, (list, tuple))
    out_specs = VMEM if single else [VMEM] * len(out_shapes)
    return pl.pallas_call(
        kernel,
        out_shape=out_shapes,
        in_specs=in_specs,
        out_specs=out_specs,
        compiler_params=pltpu.CompilerParams(vmem_limit_bytes=vmem_mib * 1024 * 1024),
    )


def shape(dims, dtype=BF16):
    return jax.ShapeDtypeStruct(dims, dtype)


def dot(a, b, contract=((1,), (0,))):
    return lax.dot_general(a, b, (contract, ((), ())), preferred_element_type=F32)


def spans(width):
    return [(start, min(CHUNK, width - start)) for start in range(0, width, CHUNK)]


def fetch(sources, held, sems):
    copies = [
        pltpu.make_async_copy(source, target, sems.at[index])
        for index, (source, target) in enumerate(zip(sources, held))
    ]
    for copy in copies:
        copy.start()
    return copies


def tail_spans(width):
    full = width // CHUNK
    return [(full * CHUNK, width - full * CHUNK)] + [
        (place * CHUNK + MAIN, TAIL) for place in range(full)
    ]


def kv_kernel(
    pos_ref, tokens_hbm, gain_hbm, key_hbm, value_hbm, normed_ref, payload_ref,
    tokens_ref, gain_ref, key_ref, value_ref, sems,
):
    sources = (tokens_hbm, gain_hbm, key_hbm, value_hbm)
    copies = fetch(sources, (tokens_ref, gain_ref, key_ref, value_ref), sems)
    rows = tokens_ref.shape[1]
    copies[0].wait()
    values = tokens_ref[...].T.astype(F32)
    mean_square = jnp.mean(values * values, axis=-1, keepdims=True)
    copies[1].wait()
    normed = (values * lax.rsqrt(mean_square + EPSILON) * gain_ref[...][None, :]).astype(BF16)
    normed_ref[...] = normed
    copies[2].wait()
    keys = dot(normed, key_ref[...], ((1,), (1,)))
    copies[3].wait()
    vals = dot(normed, value_ref[...], ((1,), (1,)))
    payload_ref[:rows, :] = jnp.concatenate([keys, vals], axis=1).astype(BF16)
    base = pos_ref[0]
    lane = lax.broadcasted_iota(jnp.int32, (EXTRA, payload_ref.shape[1]), 1)
    marks = jnp.where(lane == 0, base // 128, jnp.where(lane == 1, base % 128, 0))
    payload_ref[rows:, :] = marks.astype(F32).astype(BF16)


def project_kv(positions, tokens, gain, keys, vals):
    width, rows = tokens.shape
    arrays = (tokens, gain, keys, vals)
    return pl.pallas_call(
        kv_kernel,
        out_shape=[shape((rows, width)), shape((rows + EXTRA, 2 * HEAD_WIDTH))],
        in_specs=[SMEM] + [HBM] * 4,
        out_specs=[VMEM, VMEM],
        scratch_shapes=[pltpu.VMEM(a.shape, a.dtype) for a in arrays]
        + [pltpu.SemaphoreType.DMA((4,))],
        compiler_params=pltpu.CompilerParams(vmem_limit_bytes=32 * 1024 * 1024),
    )(in_hbm(positions), *[in_hbm(a) for a in arrays])


def query_kernel(normed_ref, w_ref, out_ref):
    rows = normed_ref.shape[0]
    heads = w_ref.shape[1] // HEAD_WIDTH
    queries = dot(normed_ref[...], w_ref[...]).astype(BF16)
    queries = queries * jnp.asarray(HEAD_WIDTH ** (-0.5), BF16)
    lane = lax.broadcasted_iota(jnp.int32, (rows, HEAD_WIDTH), 1)
    flag = jnp.where(lane == 0, 1.0, 0.0).astype(BF16)
    for head in range(heads):
        own = queries[:, head * HEAD_WIDTH:(head + 1) * HEAD_WIDTH]
        out_ref[head * rows:(head + 1) * rows, :] = jnp.concatenate([own, flag], axis=1)


def upright(ref):
    spare = jnp.zeros((8 - ref.shape[0], ref.shape[1]), F32)
    return jnp.concatenate([ref[...].astype(F32), spare], axis=0).T


def prepare_kernel(
    experts, slots, member_ref, ids_ref, weights_ref, tokens_ref, gain_ref,
    gather_ref, combine_ref, own_tokens_ref, own_gain_ref, gain_scratch,
):
    top, rows = ids_ref.shape
    cells = experts * slots
    ids, weights = upright(ids_ref), upright(weights_ref)
    expert_lane = lax.broadcasted_iota(jnp.int32, (rows, experts), 1).astype(F32)
    chosen = [(ids[:, k:k + 1] == expert_lane).astype(F32) for k in range(top)]
    named = functools.reduce(jnp.add, chosen)
    below = lax.broadcasted_iota(jnp.int32, (rows, rows), 1) < lax.broadcasted_iota(
        jnp.int32, (rows, rows), 0
    )
    place = dot(below.astype(BF16), named.astype(BF16)) + expert_lane * slots
    cell = lax.broadcasted_iota(jnp.int32, (rows, cells), 1).astype(F32)
    filled = jnp.zeros((rows, cells), F32)
    scaled = jnp.zeros((rows, cells), F32)
    for k in range(top):
        target = jnp.sum(chosen[k] * place, axis=1, keepdims=True)
        match = cell == target
        filled = jnp.where(match, 1.0, filled)
        scaled = jnp.where(match, weights[:, k:k + 1], scaled)
    gather_ref[...] = filled.T.astype(BF16)
    for part in range(3):
        rounded = scaled.astype(BF16)
        combine_ref[part * rows:(part + 1) * rows, :] = rounded
        scaled = scaled - rounded.astype(F32)

    width = tokens_ref.shape[0]
    full = width // CHUNK
    rest = width - full * CHUNK
    tails = tail_spans(width)
    spare = CHUNK - sum(size for _, size in tails)
    member = member_ref[0]
    is_last = jnp.full((1, 1), member, jnp.int32) == full
    start = pl.multiple_of(member * CHUNK, rest)
    second = pl.multiple_of(jnp.minimum(start + CHUNK - rest, full * CHUNK), rest)
    main = jnp.concatenate(
        [tokens_ref[pl.ds(start, rest), :], tokens_ref[pl.ds(second, CHUNK - rest), :]], axis=0
    ).astype(F32)
    tail = jnp.concatenate(
        [tokens_ref[first:first + size, :].astype(F32) for first, size in tails]
        + [jnp.zeros((spare, rows), F32)],
        axis=0,
    )
    feature = lax.broadcasted_iota(jnp.int32, main.shape, 0)
    own = jnp.where(is_last, tail, jnp.where(feature < MAIN, main, 0.0))
    own_tokens_ref[...] = own.T.astype(BF16)

    gain = gain_ref[...][None, :]
    gain_scratch[:, :width] = gain
    gain_scratch[:, width:] = jnp.zeros((1, gain_scratch.shape[1] - width), F32)
    main = gain_scratch[:, pl.ds(pl.multiple_of(member * CHUNK, 128), CHUNK)]
    tail = jnp.concatenate(
        [gain[:, first:first + size] for first, size in tails] + [jnp.zeros((1, spare), F32)], axis=1
    )
    feature = lax.broadcasted_iota(jnp.int32, main.shape, 1)
    own_gain_ref[...] = jnp.where(is_last, tail, jnp.where(feature < MAIN, main, 0.0))


def prepare(experts, slots, member, ids, weights, tokens, gain):
    width, rows = tokens.shape
    return pl.pallas_call(
        functools.partial(prepare_kernel, experts, slots),
        out_shape=[
            shape((experts * slots, rows)),
            shape((3 * rows, experts * slots)),
            shape((rows, CHUNK)),
            shape((1, CHUNK), F32),
        ],
        in_specs=[SMEM] + [VMEM] * 4,
        out_specs=[VMEM] * 4,
        scratch_shapes=[pltpu.VMEM((1, (width // CHUNK + 1) * CHUNK), F32)],
        compiler_params=pltpu.CompilerParams(vmem_limit_bytes=24 * 1024 * 1024),
    )(member.reshape(1), ids, weights, tokens, gain)


def attend(pos_ref, query_ref, kv_refs, carry, diagonal=False):
    rows = kv_refs[0].shape[1] - EXTRA
    mine = pos_ref[0].astype(F32)
    key_side = lax.broadcasted_iota(jnp.int32, (rows, 2 * HEAD_WIDTH), 1) < HEAD_WIDTH
    flag_lane = lax.broadcasted_iota(jnp.int32, (rows, 2 * HEAD_WIDTH), 1) == HEAD_WIDTH
    top, mixed = carry
    for _ in range(1):
        keys = []
        vals = []
        limits = []
        for kv_ref, block in [(ref, i) for ref in kv_refs for i in range(ref.shape[0])]:
            marks = kv_ref[block, rows:rows + EXTRA, :].astype(F32)
            base = marks[0:1, 0:1] * 128.0 + marks[0:1, 1:2]
            hidden = jnp.where(base <= mine, 0.0, -1e30)
            limits.append(mine - base)
            kv = kv_ref[block, :rows, :].astype(F32)
            keys.append(jnp.where(key_side, kv, jnp.where(flag_lane, hidden, 0.0)).astype(BF16))
            vals.append(jnp.where(key_side, 1.0, kv).astype(BF16))
        keys = jnp.concatenate(keys, axis=0)
        vals = jnp.concatenate(vals, axis=0)
        scores = dot(query_ref[...], keys, ((1,), (1,)))
        if diagonal:
            parts = []
            for block in range(kv_refs[0].shape[0]):
                part = scores[:, block * rows:(block + 1) * rows]
                query_row = lax.broadcasted_iota(jnp.int32, part.shape, 0) % rows
                key_row = lax.broadcasted_iota(jnp.int32, part.shape, 1)
                ahead = (key_row - query_row).astype(F32)
                parts.append(jnp.where(ahead <= limits[block], part, -1e30))
            scores = jnp.concatenate(parts + [scores[:, len(parts) * rows:]], axis=1)
        top_new = jnp.maximum(top, jnp.max(scores, axis=1, keepdims=True))
        probs = jnp.exp(scores - top_new).astype(BF16)
        mixed = mixed * jnp.exp(top - top_new) + dot(probs, vals)
        top = top_new
    return top, mixed


def first_attention_kernel(pos_ref, sink_ref, query_ref, *refs):
    *kv_refs, top_ref, mixed_ref = refs
    columns = query_ref.shape[0]
    heads = sink_ref.shape[0]
    top = jnp.concatenate(
        [jnp.full((columns // heads, 1), sink_ref[head], F32) for head in range(heads)], axis=0
    )
    lane = lax.broadcasted_iota(jnp.int32, (columns, 2 * HEAD_WIDTH), 1)
    start = (top, jnp.where(lane < HEAD_WIDTH, 1.0, 0.0))
    top_ref[...], mixed_ref[...] = attend(pos_ref, query_ref, kv_refs, start, True)


def middle_attention_kernel(pos_ref, query_ref, old_top_ref, old_mixed_ref, *refs):
    *kv_refs, top_ref, mixed_ref = refs
    carry = (old_top_ref[...], old_mixed_ref[...])
    top_ref[...], mixed_ref[...] = attend(pos_ref, query_ref, kv_refs, carry)


def last_attention_kernel(pos_ref, query_ref, old_top_ref, old_mixed_ref, w_ref, *refs):
    *kv_refs, out_ref = refs
    width = w_ref.shape[0]
    columns = query_ref.shape[0]
    rows = out_ref.shape[1]
    _, mixed = attend(pos_ref, query_ref, kv_refs, (old_top_ref[...], old_mixed_ref[...]))
    heads = (mixed[:, HEAD_WIDTH:] / mixed[:, :HEAD_WIDTH]).astype(BF16)
    stacked = jnp.concatenate(
        [heads[head * rows:(head + 1) * rows] for head in range(columns // rows)], axis=1
    )
    full = width // CHUNK
    for place in range(full):
        part = dot(stacked, w_ref[place * CHUNK:(place + 1) * CHUNK, :], ((1,), (1,)))
        out_ref[place] = part.astype(BF16)
    tail = jnp.concatenate(
        [w_ref[first:first + size, :] for first, size in tail_spans(width)], axis=0
    )
    out_ref[full] = jnp.zeros((rows, CHUNK), BF16)
    out_ref[full, :, :tail.shape[0]] = dot(stacked, tail, ((1,), (1,))).astype(BF16)


def dispatch_kernel(
    parts_ref, tokens_ref, gain_ref, gather_ref, attended_ref, residual_ref, out_ref
):
    total = parts_ref[0].astype(F32)
    for index in range(1, parts_ref.shape[0]):
        total = total + parts_ref[index].astype(F32)
    lane = lax.broadcasted_iota(jnp.int32, total.shape, 1)
    attended = jnp.where(lane < MAIN, total, 0.0).astype(BF16)
    attended_ref[...] = attended
    residual = tokens_ref[...].astype(F32) + attended.astype(F32)
    residual_ref[...] = residual
    left = jnp.sum(residual * residual, axis=1, keepdims=True)
    moe_in = residual * gain_ref[...]
    for place in range(3):
        rounded = left.astype(BF16).astype(F32)
        moe_in = jnp.where(lane == MAIN + place, rounded, moe_in)
        left = left - rounded
    out_ref[...] = dot(gather_ref[...], moe_in.astype(BF16)).astype(BF16)


def expert_kernel(
    width, rows_in_ref, gate_ref, up_ref, down_ref, far_gate_ref, far_up_ref, late_ref,
    out_ref, rows_ref, held_ref,
):
    units = gate_ref.shape[0]
    held_ref[:LATE, :] = late_ref[:LATE, :]
    held_ref[LATE:, :] = far_up_ref[...]
    own = (gate_ref, up_ref, down_ref)
    far = (far_gate_ref, held_ref, late_ref.at[pl.ds(LATE, units)])
    full = width // CHUNK
    split = CHUNK - 128
    count = rows_in_ref.shape[1]
    main_lane = lax.broadcasted_iota(jnp.int32, (count, 128), 1) < MAIN - split
    squares = jnp.zeros((count, 128), F32)
    for place in range(full + 1):
        last = rows_in_ref[place, :, split:].astype(F32)
        squares = squares + jnp.where(main_lane, 0.0, last)
        if place < full:
            first = place * CHUNK
            rows_ref[:, first:first + split] = rows_in_ref[place, :, :split]
            rows_ref[:, first + split:first + CHUNK] = jnp.where(main_lane, last, 0.0).astype(BF16)
    squares = jnp.sum(squares, axis=1, keepdims=True)
    scale = lax.rsqrt(squares / width + EPSILON)
    tails = tail_spans(width)
    tail_width = sum(size for _, size in tails)
    tail_rows = rows_in_ref[full, :, :tail_width]

    def columns(refs_in, first, size):
        start = 0
        for ref in refs_in:
            if start <= first < start + ref.shape[1]:
                return ref[:, first - start:first - start + size]
            start += ref.shape[1]

    def tail(refs_in):
        return jnp.concatenate([columns(refs_in, *span) for span in tails], axis=1)

    def product(ref):
        main = dot(rows_ref[...], ref[:, :full * CHUNK], ((1,), (1,)))
        return (main + dot(tail_rows, tail([ref]), ((1,), (1,)))) * scale

    hidden = []
    downs = []
    for gate_ref, up_ref, down_ref in (own, far):
        gate = product(gate_ref)
        up = product(up_ref)
        hidden.append((gate * jax.nn.sigmoid(1.702 * gate) * (up + 1.0)).astype(BF16))
        downs.append([down_ref])
    for place in range(full):
        part = 0.0
        for act, down in zip(hidden, downs):
            part = part + dot(act, columns(down, place * CHUNK, CHUNK))
        out_ref[place] = part.astype(BF16)
    part = 0.0
    for act, down in zip(hidden, downs):
        part = part + dot(act, tail(down))
    out_ref[full] = jnp.zeros(out_ref.shape[1:], BF16)
    out_ref[full, :, :tail_width] = part.astype(BF16)


def run_experts(width, expert_rows, own, far):
    rows = expert_rows.shape[1]
    return pl.pallas_call(
        functools.partial(expert_kernel, width),
        out_shape=shape(expert_rows.shape),
        in_specs=[VMEM] * 7,
        out_specs=VMEM,
        scratch_shapes=[
            pltpu.VMEM((rows, width // CHUNK * CHUNK), BF16),
            pltpu.VMEM(own[1].shape, BF16),
        ],
        compiler_params=pltpu.CompilerParams(vmem_limit_bytes=20 * 1024 * 1024),
    )(expert_rows, *own, *far)


def sum_kernel(groups, parts_ref, out_ref):
    for half, members in enumerate(groups):
        total = parts_ref[members[0]].astype(F32)
        for index in members[1:]:
            total = total + parts_ref[index].astype(F32)
        out_ref[half] = total.astype(BF16)


def combine_kernel(returned_ref, combine_ref, residual_ref, attended_ref, out_ref):
    rows = residual_ref.shape[0]
    mixed = dot(combine_ref[...], returned_ref[...])
    total = mixed[:rows] + mixed[rows:2 * rows] + mixed[2 * rows:]
    out_ref[:, :CHUNK] = attended_ref[...]
    out_ref[:, CHUNK:] = (residual_ref[...] + total).astype(BF16)


def finish_kernel(parts_ref, attended_ref, layer_ref):
    width = attended_ref.shape[1]
    full = width // CHUNK
    for out_ref, at in ((attended_ref, 0), (layer_ref, CHUNK)):
        last = parts_ref[full, :, at:at + CHUNK].astype(F32)
        rest = width - full * CHUNK
        for place in range(full):
            start = rest + place * TAIL
            main = parts_ref[place, :, at:at + MAIN].astype(F32)
            whole = jnp.concatenate([main, last[:, start:start + TAIL]], axis=1)
            out_ref[:, place * CHUNK:(place + 1) * CHUNK] = whole.astype(BF16)
        out_ref[:, full * CHUNK:] = last[:, :rest].astype(BF16)


def exchange(block, axis, groups=None):
    return lax.all_to_all(
        block, axis, split_axis=0, concat_axis=0, tiled=True, axis_index_groups=groups
    )


def local(
    tokens,
    positions,
    norm_attn,
    norm_moe,
    w_query,
    key_matrix,
    value_matrix,
    w_out,
    sinks,
    expert_ids,
    expert_weights,
    w_gate,
    w_up,
    w_down,
):
    ctx_count = lax.axis_size("ctx")
    exp_count = lax.axis_size("exp")
    rows, width = tokens.shape
    heads = sinks.shape[0]
    top = expert_ids.shape[1]
    experts = ctx_count
    slots = rows * top * 3 // (2 * experts)
    member = lax.axis_index("exp")

    swap = [(i, i ^ 2) for i in range(exp_count)]
    gate, up, down = w_gate[0].T, w_up[0].T, w_down[0]

    normed, payload = project_kv(
        positions, tokens.T, norm_attn, key_matrix.T, value_matrix.T
    )
    far_gate = lax.ppermute(gate, "exp", swap)
    late = jnp.concatenate([up[:LATE], down], axis=0)

    def moved(block, x, z, core):
        route = []
        for i in range(ctx_count):
            there = (i // 8 + x) % 4 * 8 + (i // 2 % 4 + z) % 4 * 2 + (i % 2 + core) % 2
            route.append((i, there))
        return lax.ppermute(block, "ctx", route)

    queries = call(query_kernel, shape((heads * rows, 2 * HEAD_WIDTH)), [VMEM, VMEM])(normed, w_query)
    lines = [
        [i for i in range(ctx_count) if i // 8 == x and i % 2 == core]
        for x in range(ctx_count // 8)
        for core in range(2)
    ]
    copies = jnp.broadcast_to(payload[None], (len(lines[0]),) + payload.shape)
    column = exchange(copies, "ctx", lines)
    column, queries = lax.optimization_barrier((column, queries))
    column_far = moved(column, 0, 0, 1)
    planes = [moved(column, x, 0, 0) for x in range(1, 4)]
    state = [shape((heads * rows, 1), F32), shape((heads * rows, 2 * HEAD_WIDTH), F32)]
    carried = call(first_attention_kernel, state, [SMEM, SMEM] + [VMEM] * 3)(
        positions, sinks, queries, column, column_far
    )
    prepared = prepare(
        experts, slots, member, expert_ids.T, expert_weights.T, tokens.T, norm_moe
    )
    *planes, top_row, mixed, gather_table, combine_table, own_tokens, own_gain, late = (
        lax.optimization_barrier((*planes, *carried, *prepared, late))
    )
    planes_far = [moved(plane, 0, 0, 1) for plane in planes]
    carried = call(middle_attention_kernel, state, [SMEM] + [VMEM] * 6)(
        positions, queries, top_row, mixed, *planes
    )
    top_row, mixed, far_gate = lax.optimization_barrier((*carried, far_gate))
    far_up = lax.ppermute(up[LATE:], "exp", swap)
    partial_sums = call(
        last_attention_kernel, shape((exp_count, rows, CHUNK)), [SMEM] + [VMEM] * 7
    )(positions, queries, top_row, mixed, w_out.T, *planes_far)
    partial_sums, far_up, late = lax.optimization_barrier((partial_sums, far_up, late))
    parts = exchange(partial_sums, "exp")
    attended, residual, outgoing = call(
        dispatch_kernel,
        [shape((rows, CHUNK)), shape((rows, CHUNK), F32), shape((experts * slots, CHUNK))],
        [VMEM] * 4,
    )(parts, own_tokens, own_gain, gather_table)
    arrived = exchange(outgoing.reshape(ctx_count, slots, CHUNK), "ctx")
    far_late = lax.ppermute(late, "exp", swap)
    arrived, far_late = lax.optimization_barrier((arrived, far_late))
    halves = arrived.reshape(1, 2, 1, ctx_count * slots // 2, CHUNK)
    spread = jnp.broadcast_to(halves, (exp_count // 4, 2, 2) + halves.shape[3:])
    expert_rows = exchange(spread.reshape((exp_count,) + halves.shape[3:]), "exp")
    products = run_experts(width, expert_rows, (gate, up, down), (far_gate, far_up, far_late))
    product_parts = exchange(products, "exp")
    groups = [[i for i in range(exp_count) if (i >> 1) & 1 == half] for half in range(2)]
    summed = call(
        functools.partial(sum_kernel, groups),
        shape((2, ctx_count * slots // 2, CHUNK)),
        [VMEM],
    )(product_parts)
    returned = exchange(summed.reshape(ctx_count, slots, CHUNK), "ctx")
    final = call(combine_kernel, shape((rows, 2 * CHUNK)), [VMEM] * 4)(
        returned.reshape(experts * slots, CHUNK), combine_table, residual, attended
    )
    final = exchange(final.reshape(exp_count, rows // exp_count, 2 * CHUNK), "exp")
    out = shape((rows // exp_count, width))
    return tuple(call(finish_kernel, [out, out], [VMEM])(final))


def solution(mesh):
    in_specs = (
        P("ctx", None),
        P("ctx"),
        P(),
        P(),
        P(None, "exp"),
        P(None, "exp"),
        P(None, "exp"),
        P("exp", None),
        P("exp"),
        P("ctx", None),
        P("ctx", None),
        P("ctx", None, "exp"),
        P("ctx", None, "exp"),
        P("ctx", "exp", None),
    )
    out_specs = (P(("ctx", "exp"), None), P(("ctx", "exp"), None))
    return jax.shard_map(local, mesh=mesh, in_specs=in_specs, out_specs=out_specs, check_vma=False)
```

```python
import functools

import jax
import jax.numpy as jnp
from jax import lax
from jax.experimental import pallas as pl
from jax.experimental.pallas import tpu as pltpu
from jax.sharding import PartitionSpec as P

HEAD_WIDTH = 64
EPSILON = 1e-05
CHUNK = 384
TAIL = 16
LATE = 48
MAIN = CHUNK - TAIL
EXTRA = 16
BF16 = jnp.bfloat16
F32 = jnp.float32
VMEM = pl.BlockSpec(memory_space=pltpu.VMEM)
SMEM = pl.BlockSpec(memory_space=pltpu.SMEM)
HBM = pl.BlockSpec(memory_space=pltpu.HBM)


def in_hbm(array):
    return pltpu.with_memory_space_constraint(array, pltpu.HBM)


def call(kernel, out_shapes, in_specs, vmem_mib=24):
    single = not isinstance(out_shapes, (list, tuple))
    out_specs = VMEM if single else [VMEM] * len(out_shapes)
    return pl.pallas_call(
        kernel,
        out_shape=out_shapes,
        in_specs=in_specs,
        out_specs=out_specs,
        compiler_params=pltpu.CompilerParams(vmem_limit_bytes=vmem_mib * 1024 * 1024),
    )


def shape(dims, dtype=BF16):
    return jax.ShapeDtypeStruct(dims, dtype)


def dot(a, b, contract=((1,), (0,))):
    return lax.dot_general(a, b, (contract, ((), ())), preferred_element_type=F32)


def spans(width):
    return [(start, min(CHUNK, width - start)) for start in range(0, width, CHUNK)]


def fetch(sources, held, sems):
    copies = [
        pltpu.make_async_copy(source, target, sems.at[index])
        for index, (source, target) in enumerate(zip(sources, held))
    ]
    for copy in copies:
        copy.start()
    return copies


def tail_spans(width):
    full = width // CHUNK
    return [(full * CHUNK, width - full * CHUNK)] + [
        (place * CHUNK + MAIN, TAIL) for place in range(full)
    ]


def kv_kernel(
    pos_ref, tokens_hbm, gain_hbm, key_hbm, value_hbm, normed_ref, payload_ref,
    tokens_ref, gain_ref, key_ref, value_ref, sems,
):
    sources = (tokens_hbm, gain_hbm, key_hbm, value_hbm)
    copies = fetch(sources, (tokens_ref, gain_ref, key_ref, value_ref), sems)
    rows = tokens_ref.shape[1]
    copies[0].wait()
    values = tokens_ref[...].T.astype(F32)
    mean_square = jnp.mean(values * values, axis=-1, keepdims=True)
    copies[1].wait()
    normed = (values * lax.rsqrt(mean_square + EPSILON) * gain_ref[...][None, :]).astype(BF16)
    normed_ref[...] = normed
    copies[2].wait()
    keys = dot(normed, key_ref[...], ((1,), (1,)))
    copies[3].wait()
    vals = dot(normed, value_ref[...], ((1,), (1,)))
    payload_ref[:rows, :] = jnp.concatenate([keys, vals], axis=1).astype(BF16)
    base = pos_ref[0]
    lane = lax.broadcasted_iota(jnp.int32, (EXTRA, payload_ref.shape[1]), 1)
    marks = jnp.where(lane == 0, base // 128, jnp.where(lane == 1, base % 128, 0))
    payload_ref[rows:, :] = marks.astype(F32).astype(BF16)


def project_kv(positions, tokens, gain, keys, vals):
    width, rows = tokens.shape
    arrays = (tokens, gain, keys, vals)
    return pl.pallas_call(
        kv_kernel,
        out_shape=[shape((rows, width)), shape((rows + EXTRA, 2 * HEAD_WIDTH))],
        in_specs=[SMEM] + [HBM] * 4,
        out_specs=[VMEM, VMEM],
        scratch_shapes=[pltpu.VMEM(a.shape, a.dtype) for a in arrays]
        + [pltpu.SemaphoreType.DMA((4,))],
        compiler_params=pltpu.CompilerParams(vmem_limit_bytes=32 * 1024 * 1024),
    )(in_hbm(positions), *[in_hbm(a) for a in arrays])


def query_kernel(normed_ref, w_ref, out_ref):
    rows = normed_ref.shape[0]
    heads = w_ref.shape[1] // HEAD_WIDTH
    queries = dot(normed_ref[...], w_ref[...]).astype(BF16)
    queries = queries * jnp.asarray(HEAD_WIDTH ** (-0.5), BF16)
    lane = lax.broadcasted_iota(jnp.int32, (rows, HEAD_WIDTH), 1)
    flag = jnp.where(lane == 0, 1.0, 0.0).astype(BF16)
    for head in range(heads):
        own = queries[:, head * HEAD_WIDTH:(head + 1) * HEAD_WIDTH]
        out_ref[head * rows:(head + 1) * rows, :] = jnp.concatenate([own, flag], axis=1)


def upright(ref):
    spare = jnp.zeros((8 - ref.shape[0], ref.shape[1]), F32)
    return jnp.concatenate([ref[...].astype(F32), spare], axis=0).T


def prepare_kernel(
    experts, slots, member_ref, ids_ref, weights_ref, tokens_ref, gain_ref,
    gather_ref, combine_ref, own_tokens_ref, own_gain_ref, gain_scratch,
):
    top, rows = ids_ref.shape
    cells = experts * slots
    ids, weights = upright(ids_ref), upright(weights_ref)
    expert_lane = lax.broadcasted_iota(jnp.int32, (rows, experts), 1).astype(F32)
    chosen = [(ids[:, k:k + 1] == expert_lane).astype(F32) for k in range(top)]
    named = functools.reduce(jnp.add, chosen)
    below = lax.broadcasted_iota(jnp.int32, (rows, rows), 1) < lax.broadcasted_iota(
        jnp.int32, (rows, rows), 0
    )
    place = dot(below.astype(BF16), named.astype(BF16)) + expert_lane * slots
    cell = lax.broadcasted_iota(jnp.int32, (rows, cells), 1).astype(F32)
    filled = jnp.zeros((rows, cells), F32)
    scaled = jnp.zeros((rows, cells), F32)
    for k in range(top):
        target = jnp.sum(chosen[k] * place, axis=1, keepdims=True)
        match = cell == target
        filled = jnp.where(match, 1.0, filled)
        scaled = jnp.where(match, weights[:, k:k + 1], scaled)
    gather_ref[...] = filled.T.astype(BF16)
    for part in range(3):
        rounded = scaled.astype(BF16)
        combine_ref[part * rows:(part + 1) * rows, :] = rounded
        scaled = scaled - rounded.astype(F32)

    width = tokens_ref.shape[0]
    full = width // CHUNK
    rest = width - full * CHUNK
    tails = tail_spans(width)
    spare = CHUNK - sum(size for _, size in tails)
    member = member_ref[0]
    is_last = jnp.full((1, 1), member, jnp.int32) == full
    start = pl.multiple_of(member * CHUNK, rest)
    second = pl.multiple_of(jnp.minimum(start + CHUNK - rest, full * CHUNK), rest)
    main = jnp.concatenate(
        [tokens_ref[pl.ds(start, rest), :], tokens_ref[pl.ds(second, CHUNK - rest), :]], axis=0
    ).astype(F32)
    tail = jnp.concatenate(
        [tokens_ref[first:first + size, :].astype(F32) for first, size in tails]
        + [jnp.zeros((spare, rows), F32)],
        axis=0,
    )
    feature = lax.broadcasted_iota(jnp.int32, main.shape, 0)
    own = jnp.where(is_last, tail, jnp.where(feature < MAIN, main, 0.0))
    own_tokens_ref[...] = own.T.astype(BF16)

    gain = gain_ref[...][None, :]
    gain_scratch[:, :width] = gain
    gain_scratch[:, width:] = jnp.zeros((1, gain_scratch.shape[1] - width), F32)
    main = gain_scratch[:, pl.ds(pl.multiple_of(member * CHUNK, 128), CHUNK)]
    tail = jnp.concatenate(
        [gain[:, first:first + size] for first, size in tails] + [jnp.zeros((1, spare), F32)], axis=1
    )
    feature = lax.broadcasted_iota(jnp.int32, main.shape, 1)
    own_gain_ref[...] = jnp.where(is_last, tail, jnp.where(feature < MAIN, main, 0.0))


def prepare(experts, slots, member, ids, weights, tokens, gain):
    width, rows = tokens.shape
    return pl.pallas_call(
        functools.partial(prepare_kernel, experts, slots),
        out_shape=[
            shape((experts * slots, rows)),
            shape((3 * rows, experts * slots)),
            shape((rows, CHUNK)),
            shape((1, CHUNK), F32),
        ],
        in_specs=[SMEM] + [VMEM] * 4,
        out_specs=[VMEM] * 4,
        scratch_shapes=[pltpu.VMEM((1, (width // CHUNK + 1) * CHUNK), F32)],
        compiler_params=pltpu.CompilerParams(vmem_limit_bytes=24 * 1024 * 1024),
    )(member.reshape(1), ids, weights, tokens, gain)


def attend(pos_ref, query_ref, kv_refs, carry, diagonal=False):
    rows = kv_refs[0].shape[1] - EXTRA
    mine = pos_ref[0].astype(F32)
    key_side = lax.broadcasted_iota(jnp.int32, (rows, 2 * HEAD_WIDTH), 1) < HEAD_WIDTH
    flag_lane = lax.broadcasted_iota(jnp.int32, (rows, 2 * HEAD_WIDTH), 1) == HEAD_WIDTH
    top, mixed = carry
    for _ in range(1):
        keys = []
        vals = []
        limits = []
        for kv_ref, block in [(ref, i) for ref in kv_refs for i in range(ref.shape[0])]:
            marks = kv_ref[block, rows:rows + EXTRA, :].astype(F32)
            base = marks[0:1, 0:1] * 128.0 + marks[0:1, 1:2]
            hidden = jnp.where(base <= mine, 0.0, -1e30)
            limits.append(mine - base)
            kv = kv_ref[block, :rows, :].astype(F32)
            keys.append(jnp.where(key_side, kv, jnp.where(flag_lane, hidden, 0.0)).astype(BF16))
            vals.append(jnp.where(key_side, 1.0, kv).astype(BF16))
        keys = jnp.concatenate(keys, axis=0)
        vals = jnp.concatenate(vals, axis=0)
        scores = dot(query_ref[...], keys, ((1,), (1,)))
        if diagonal:
            parts = []
            for block in range(kv_refs[0].shape[0]):
                part = scores[:, block * rows:(block + 1) * rows]
                query_row = lax.broadcasted_iota(jnp.int32, part.shape, 0) % rows
                key_row = lax.broadcasted_iota(jnp.int32, part.shape, 1)
                ahead = (key_row - query_row).astype(F32)
                parts.append(jnp.where(ahead <= limits[block], part, -1e30))
            scores = jnp.concatenate(parts + [scores[:, len(parts) * rows:]], axis=1)
        top_new = jnp.maximum(top, jnp.max(scores, axis=1, keepdims=True))
        probs = jnp.exp(scores - top_new).astype(BF16)
        mixed = mixed * jnp.exp(top - top_new) + dot(probs, vals)
        top = top_new
    return top, mixed


def first_attention_kernel(pos_ref, sink_ref, query_ref, *refs):
    *kv_refs, top_ref, mixed_ref = refs
    columns = query_ref.shape[0]
    heads = sink_ref.shape[0]
    top = jnp.concatenate(
        [jnp.full((columns // heads, 1), sink_ref[head], F32) for head in range(heads)], axis=0
    )
    lane = lax.broadcasted_iota(jnp.int32, (columns, 2 * HEAD_WIDTH), 1)
    start = (top, jnp.where(lane < HEAD_WIDTH, 1.0, 0.0))
    top_ref[...], mixed_ref[...] = attend(pos_ref, query_ref, kv_refs, start, True)


def middle_attention_kernel(pos_ref, query_ref, old_top_ref, old_mixed_ref, *refs):
    *kv_refs, top_ref, mixed_ref = refs
    carry = (old_top_ref[...], old_mixed_ref[...])
    top_ref[...], mixed_ref[...] = attend(pos_ref, query_ref, kv_refs, carry)


def last_attention_kernel(pos_ref, query_ref, old_top_ref, old_mixed_ref, w_ref, *refs):
    *kv_refs, out_hbm, out_ref, sems = refs
    width = w_ref.shape[0]
    columns = query_ref.shape[0]
    rows = out_ref.shape[1]
    _, mixed = attend(pos_ref, query_ref, kv_refs, (old_top_ref[...], old_mixed_ref[...]))
    heads = (mixed[:, HEAD_WIDTH:] / mixed[:, :HEAD_WIDTH]).astype(BF16)
    stacked = jnp.concatenate(
        [heads[head * rows:(head + 1) * rows] for head in range(columns // rows)], axis=1
    )
    full = width // CHUNK
    copies = [
        pltpu.make_async_copy(out_ref.at[place], out_hbm.at[place], sems.at[place])
        for place in range(full + 1)
    ]
    tail = jnp.concatenate(
        [w_ref[first:first + size, :] for first, size in tail_spans(width)], axis=0
    )
    out_ref[full] = jnp.zeros((rows, CHUNK), BF16)
    out_ref[full, :, :tail.shape[0]] = dot(stacked, tail, ((1,), (1,))).astype(BF16)
    copies[full].start()
    for place in range(full):
        part = dot(stacked, w_ref[place * CHUNK:(place + 1) * CHUNK, :], ((1,), (1,)))
        out_ref[place] = part.astype(BF16)
        copies[place].start()
    for copy in copies:
        copy.wait()


def finish_attention(dims, operands):
    return pl.pallas_call(
        last_attention_kernel,
        out_shape=pltpu.HBM(dims, BF16),
        in_specs=[SMEM] + [VMEM] * (len(operands) - 1),
        out_specs=HBM,
        scratch_shapes=[pltpu.VMEM(dims, BF16), pltpu.SemaphoreType.DMA((dims[0],))],
        compiler_params=pltpu.CompilerParams(vmem_limit_bytes=24 * 1024 * 1024),
    )(*operands)


def dispatch_kernel(
    parts_ref, tokens_ref, gain_ref, gather_ref, attended_ref, residual_ref, out_ref
):
    total = parts_ref[0].astype(F32)
    for index in range(1, parts_ref.shape[0]):
        total = total + parts_ref[index].astype(F32)
    lane = lax.broadcasted_iota(jnp.int32, total.shape, 1)
    attended = jnp.where(lane < MAIN, total, 0.0).astype(BF16)
    attended_ref[...] = attended
    residual = tokens_ref[...].astype(F32) + attended.astype(F32)
    residual_ref[...] = residual
    left = jnp.sum(residual * residual, axis=1, keepdims=True)
    moe_in = residual * gain_ref[...]
    for place in range(3):
        rounded = left.astype(BF16).astype(F32)
        moe_in = jnp.where(lane == MAIN + place, rounded, moe_in)
        left = left - rounded
    out_ref[...] = dot(gather_ref[...], moe_in.astype(BF16)).astype(BF16)


def expert_kernel(
    width, rows_in_ref, gate_ref, up_ref, down_ref, far_gate_ref, far_up_ref, late_ref,
    out_ref, rows_ref, held_ref,
):
    units = gate_ref.shape[0]
    held_ref[:LATE, :] = late_ref[:LATE, :]
    held_ref[LATE:, :] = far_up_ref[...]
    own = (gate_ref, up_ref, down_ref)
    far = (far_gate_ref, held_ref, late_ref.at[pl.ds(LATE, units)])
    full = width // CHUNK
    split = CHUNK - 128
    count = rows_in_ref.shape[1]
    main_lane = lax.broadcasted_iota(jnp.int32, (count, 128), 1) < MAIN - split
    squares = jnp.zeros((count, 128), F32)
    for place in range(full + 1):
        last = rows_in_ref[place, :, split:].astype(F32)
        squares = squares + jnp.where(main_lane, 0.0, last)
        if place < full:
            first = place * CHUNK
            rows_ref[:, first:first + split] = rows_in_ref[place, :, :split]
            rows_ref[:, first + split:first + CHUNK] = jnp.where(main_lane, last, 0.0).astype(BF16)
    squares = jnp.sum(squares, axis=1, keepdims=True)
    scale = lax.rsqrt(squares / width + EPSILON)
    tails = tail_spans(width)
    tail_width = sum(size for _, size in tails)
    tail_rows = rows_in_ref[full, :, :tail_width]

    def columns(refs_in, first, size):
        start = 0
        for ref in refs_in:
            if start <= first < start + ref.shape[1]:
                return ref[:, first - start:first - start + size]
            start += ref.shape[1]

    def tail(refs_in):
        return jnp.concatenate([columns(refs_in, *span) for span in tails], axis=1)

    def product(ref):
        main = dot(rows_ref[...], ref[:, :full * CHUNK], ((1,), (1,)))
        return (main + dot(tail_rows, tail([ref]), ((1,), (1,)))) * scale

    hidden = []
    downs = []
    for gate_ref, up_ref, down_ref in (own, far):
        gate = product(gate_ref)
        up = product(up_ref)
        hidden.append((gate * jax.nn.sigmoid(1.702 * gate) * (up + 1.0)).astype(BF16))
        downs.append([down_ref])
    for place in range(full):
        part = 0.0
        for act, down in zip(hidden, downs):
            part = part + dot(act, columns(down, place * CHUNK, CHUNK))
        out_ref[place] = part.astype(BF16)
    part = 0.0
    for act, down in zip(hidden, downs):
        part = part + dot(act, tail(down))
    out_ref[full] = jnp.zeros(out_ref.shape[1:], BF16)
    out_ref[full, :, :tail_width] = part.astype(BF16)


def run_experts(width, expert_rows, own, far):
    rows = expert_rows.shape[1]
    return pl.pallas_call(
        functools.partial(expert_kernel, width),
        out_shape=shape(expert_rows.shape),
        in_specs=[VMEM] * 7,
        out_specs=VMEM,
        scratch_shapes=[
            pltpu.VMEM((rows, width // CHUNK * CHUNK), BF16),
            pltpu.VMEM(own[1].shape, BF16),
        ],
        compiler_params=pltpu.CompilerParams(vmem_limit_bytes=20 * 1024 * 1024),
    )(expert_rows, *own, *far)


def sum_kernel(groups, parts_ref, out_ref):
    for half, members in enumerate(groups):
        total = parts_ref[members[0]].astype(F32)
        for index in members[1:]:
            total = total + parts_ref[index].astype(F32)
        out_ref[half] = total.astype(BF16)


def combine_kernel(returned_ref, combine_ref, residual_ref, attended_ref, out_ref):
    rows = residual_ref.shape[0]
    mixed = dot(combine_ref[...], returned_ref[...])
    total = mixed[:rows] + mixed[rows:2 * rows] + mixed[2 * rows:]
    out_ref[:, :CHUNK] = attended_ref[...]
    out_ref[:, CHUNK:] = (residual_ref[...] + total).astype(BF16)


def finish_kernel(parts_ref, attended_ref, layer_ref):
    width = attended_ref.shape[1]
    full = width // CHUNK
    for out_ref, at in ((attended_ref, 0), (layer_ref, CHUNK)):
        last = parts_ref[full, :, at:at + CHUNK].astype(F32)
        rest = width - full * CHUNK
        for place in range(full):
            start = rest + place * TAIL
            main = parts_ref[place, :, at:at + MAIN].astype(F32)
            whole = jnp.concatenate([main, last[:, start:start + TAIL]], axis=1)
            out_ref[:, place * CHUNK:(place + 1) * CHUNK] = whole.astype(BF16)
        out_ref[:, full * CHUNK:] = last[:, :rest].astype(BF16)


def exchange(block, axis, groups=None):
    return lax.all_to_all(
        block, axis, split_axis=0, concat_axis=0, tiled=True, axis_index_groups=groups
    )


def local(
    tokens,
    positions,
    norm_attn,
    norm_moe,
    w_query,
    key_matrix,
    value_matrix,
    w_out,
    sinks,
    expert_ids,
    expert_weights,
    w_gate,
    w_up,
    w_down,
):
    ctx_count = lax.axis_size("ctx")
    exp_count = lax.axis_size("exp")
    rows, width = tokens.shape
    heads = sinks.shape[0]
    top = expert_ids.shape[1]
    experts = ctx_count
    slots = rows * top * 3 // (2 * experts)
    member = lax.axis_index("exp")

    swap = [(i, i ^ 2) for i in range(exp_count)]
    gate, up, down = w_gate[0].T, w_up[0].T, w_down[0]

    normed, payload = project_kv(
        positions, tokens.T, norm_attn, key_matrix.T, value_matrix.T
    )
    far_gate = lax.ppermute(gate, "exp", swap)
    late = jnp.concatenate([up[:LATE], down], axis=0)

    def moved(block, x, z, core):
        route = []
        for i in range(ctx_count):
            there = (i // 8 + x) % 4 * 8 + (i // 2 % 4 + z) % 4 * 2 + (i % 2 + core) % 2
            route.append((i, there))
        return lax.ppermute(block, "ctx", route)

    queries = call(query_kernel, shape((heads * rows, 2 * HEAD_WIDTH)), [VMEM, VMEM])(normed, w_query)
    lines = [
        [i for i in range(ctx_count) if i // 8 == x and i % 2 == core]
        for x in range(ctx_count // 8)
        for core in range(2)
    ]
    copies = jnp.broadcast_to(payload[None], (len(lines[0]),) + payload.shape)
    column = exchange(copies, "ctx", lines)
    column, queries = lax.optimization_barrier((column, queries))
    column_far = moved(column, 0, 0, 1)
    planes = [moved(column, x, 0, 0) for x in range(1, 4)]
    state = [shape((heads * rows, 1), F32), shape((heads * rows, 2 * HEAD_WIDTH), F32)]
    carried = call(first_attention_kernel, state, [SMEM, SMEM] + [VMEM] * 3)(
        positions, sinks, queries, column, column_far
    )
    prepared = prepare(
        experts, slots, member, expert_ids.T, expert_weights.T, tokens.T, norm_moe
    )
    *planes, top_row, mixed, gather_table, combine_table, own_tokens, own_gain, late = (
        lax.optimization_barrier((*planes, *carried, *prepared, late))
    )
    planes_far = [moved(plane, 0, 0, 1) for plane in planes]
    carried = call(middle_attention_kernel, state, [SMEM] + [VMEM] * 6)(
        positions, queries, top_row, mixed, *planes
    )
    top_row, mixed, far_gate = lax.optimization_barrier((*carried, far_gate))
    far_up = lax.ppermute(up[LATE:], "exp", swap)
    operands = (positions, queries, top_row, mixed, w_out.T, *planes_far)
    partial_sums = finish_attention((exp_count, rows, CHUNK), operands)
    partial_sums, far_up, late = lax.optimization_barrier((partial_sums, far_up, late))
    parts = exchange(partial_sums, "exp")
    attended, residual, outgoing = call(
        dispatch_kernel,
        [
            pltpu.HBM((rows, CHUNK), BF16),
            shape((rows, CHUNK), F32),
            shape((experts * slots, CHUNK)),
        ],
        [VMEM] * 4,
    )(parts, own_tokens, own_gain, gather_table)
    arrived = exchange(outgoing.reshape(ctx_count, slots, CHUNK), "ctx")
    far_late = lax.ppermute(late, "exp", swap)
    arrived, far_late = lax.optimization_barrier((arrived, far_late))
    halves = arrived.reshape(1, 2, 1, ctx_count * slots // 2, CHUNK)
    spread = jnp.broadcast_to(halves, (exp_count // 4, 2, 2) + halves.shape[3:])
    expert_rows = exchange(spread.reshape((exp_count,) + halves.shape[3:]), "exp")
    products = run_experts(width, expert_rows, (gate, up, down), (far_gate, far_up, far_late))
    product_parts = exchange(products, "exp")
    groups = [[i for i in range(exp_count) if (i >> 1) & 1 == half] for half in range(2)]
    summed = call(
        functools.partial(sum_kernel, groups),
        shape((2, ctx_count * slots // 2, CHUNK)),
        [VMEM],
    )(product_parts)
    returned = exchange(summed.reshape(ctx_count, slots, CHUNK), "ctx")
    final = call(combine_kernel, shape((rows, 2 * CHUNK)), [VMEM] * 4)(
        returned.reshape(experts * slots, CHUNK), combine_table, residual, attended
    )
    final = exchange(final.reshape(exp_count, rows // exp_count, 2 * CHUNK), "exp")
    out = shape((rows // exp_count, width))
    return tuple(call(finish_kernel, [out, out], [VMEM])(final))


def solution(mesh):
    in_specs = (
        P("ctx", None),
        P("ctx"),
        P(),
        P(),
        P(None, "exp"),
        P(None, "exp"),
        P(None, "exp"),
        P("exp", None),
        P("exp"),
        P("ctx", None),
        P("ctx", None),
        P("ctx", None, "exp"),
        P("ctx", None, "exp"),
        P("ctx", "exp", None),
    )
    out_specs = (P(("ctx", "exp"), None), P(("ctx", "exp"), None))
    return jax.shard_map(local, mesh=mesh, in_specs=in_specs, out_specs=out_specs, check_vma=False)
```
